256 devices in a mesh: queue: 8 (over x, core), seq: 32 (over z, y).
Axes of the slice: x: 4, y: 4, z: 8, core: 2. Of those that a mesh axis runs over, the one named last changes fastest.
Arguments:
- hidden: bfloat16 [8, 1536, 3072], P('queue', 'seq'), may hold values from -1.1953125 to 1.1953125
- queries: bfloat16 [8, 1536, 2048], P('queue', 'seq'), may hold values from -64 to 64
- keys: bfloat16 [8, 1536, 2048], P('queue', 'seq'), may hold values from -30 to 30
- values: bfloat16 [8, 1536, 2048], P('queue', 'seq'), may hold values from -6 to 6
- timesteps: int32 [8], P('queue'), may hold values from 125 to 1000, as said below
- latents: float32 [8, 1536, 64], P('queue', 'seq'), may hold values from -6 to 6
- fresh_noise: float32 [1536, 64], P('seq'), may hold values from -6 to 6
- out_weight: bfloat16 [2048, 3072], P('seq'), may hold values from -0.125 to 0.125
- mod_weight: bfloat16 [256, 9216], replicated, may hold values from -0.75 to 0.75
- final_weight: bfloat16 [3072, 64], replicated, may hold values from -0.109375 to 0.109375
Outputs:
- velocity: float32 [8, 1536, 64], P('queue', 'seq')
- next_latents: float32 [8, 1536, 64], P('queue', 'seq')
The draws below stay inside these ranges and needn't reach their ends.
Inputs may be any that keep to these rules, and one draw needn't show every extreme that they name: timesteps fall strictly along the queue: the first block's is 1000 and the last block's is 125.
All inputs are finite; a program needn't handle non-finite values.
Results may differ from the reference program's by a relative error of at most 0.008.
Values may be sent and summed in bfloat16 or wider, within the bound.
A program may use at most 128 MiB of HBM per device.

```python
import math
import jax
import jax.numpy as jnp
from jax import lax

D = 3072
H = 16
DH = 128
TEMB = 256
C_LAT = 64
STRIDE = 125
SPAN = 1536
QUEUE_LEN = 8
HD = 2048


def draw_queries(key, part):
    key = jax.random.fold_in(key, 11)
    result = 2.5 * jax.random.normal(key, (QUEUE_LEN, SPAN, H * DH), jnp.float32)
    return jnp.clip(result, -64.0, 64.0).astype(jnp.bfloat16)


def draw_keys(key, part):
    key = jax.random.fold_in(key, 23)
    result = jax.random.normal(key, (QUEUE_LEN, SPAN, H * DH), jnp.float32)
    return jnp.clip(result, -30.0, 30.0).astype(jnp.bfloat16)


def draw_timesteps(key, part):
    key = jax.random.fold_in(key, 37)
    place = jnp.arange(QUEUE_LEN, dtype=jnp.int32)
    base_steps = 1000 - place * (1000 - STRIDE) // max(QUEUE_LEN - 1, 1)
    jitter = jax.random.randint(key, (QUEUE_LEN,), 0, STRIDE, dtype=jnp.int32)
    inner = (place > 0) & (place < QUEUE_LEN - 1)
    return (base_steps - jnp.where(inner, jitter, 0)).astype(jnp.int32)


def shard_levels(rng, shape, pieces, smallest, largest):
    factor_of, own = 1.0, jax.random.fold_in(rng, 6)
    for dim, shards_of in pieces:
        draws = jnp.exp(jax.random.uniform(jax.random.fold_in(own, dim), (shards_of,), jnp.float32, smallest / len(pieces), largest / len(pieces)))
        factor_of = factor_of * jnp.repeat(draws, shape[dim] // shards_of).reshape([-1 if axis == dim else 1 for axis in range(len(shape))])
    return factor_of


def scatter_about(stream_key, shape, scale, most, cuts=(), kind=jnp.bfloat16):
    array = scale * jax.random.normal(stream_key, shape, jnp.float32)
    if cuts:
        array = array * shard_levels(stream_key, shape, cuts, -0.22, 0.18)
    return jnp.clip(array, -most, most).astype(kind)


def setup_inputs(seed: int = 0) -> dict:
    arg_keys = jax.random.split(jax.random.key(seed), 11)
    return {
        "hidden": scatter_about(arg_keys[0], (QUEUE_LEN, SPAN, D), 0.2, 1.1953125, ((0, 8), (1, 32))),
        "queries": draw_queries(jax.random.fold_in(arg_keys[10], 71), 0),
        "keys": draw_keys(jax.random.fold_in(arg_keys[10], 71), 0),
        "values": scatter_about(arg_keys[3], (QUEUE_LEN, SPAN, HD), 1.0, 6.0, ((0, 8), (1, 32))),
        "timesteps": draw_timesteps(jax.random.fold_in(arg_keys[10], 71), 0),
        "latents": scatter_about(arg_keys[5], (QUEUE_LEN, SPAN, C_LAT), 1.0, 6.0, ((0, 8), (1, 32)), jnp.float32),
        "fresh_noise": scatter_about(arg_keys[6], (SPAN, C_LAT), 1.0, 6.0, ((0, 32),), jnp.float32),
        "out_weight": scatter_about(arg_keys[7], (HD, D), HD ** -0.5, 0.125, ((0, 32),)),
        "mod_weight": scatter_about(arg_keys[8], (TEMB, 3 * D), 0.125, 0.75),
        "final_weight": scatter_about(arg_keys[9], (D, C_LAT), D ** -0.5, 0.109375),
    }


def time_embed(step_values):
    halfway = TEMB // 2
    freqs = jnp.exp(-math.log(10000.0) * jnp.arange(halfway, dtype=jnp.float32) / halfway)
    angles = step_values.astype(jnp.float32)[:, None] * freqs[None, :]
    return jnp.concatenate([jnp.cos(angles), jnp.sin(angles)], axis=1)

def split_heads(rows):
    return rows.reshape(rows.shape[0], H, DH).transpose(1, 0, 2)

def head_attention(operands):
    query_head, key_head, value_head = operands
    scores = jnp.dot(query_head, key_head.T, preferred_element_type=jnp.float32) * DH ** (-0.5)
    peak = lax.optimization_barrier(jnp.max(scores, axis=1, keepdims=True))
    weights = jnp.exp(scores - peak)
    totals = lax.optimization_barrier(jnp.sum(weights, axis=1, keepdims=True))
    mixed = jnp.dot(weights.astype(jnp.bfloat16), value_head, preferred_element_type=jnp.float32)
    return (mixed / totals).astype(jnp.bfloat16)

def reference(hidden, queries, keys, values, timesteps, latents, fresh_noise, out_weight, mod_weight, final_weight):
    embed = time_embed(timesteps)
    activated = jax.nn.silu(embed).astype(jnp.bfloat16)
    modulation = jnp.dot(activated, mod_weight, preferred_element_type=jnp.float32)
    velocity_list = []
    updated_list = []
    for group in range(QUEUE_LEN):
        gate = modulation[group, :D]
        shift = modulation[group, D:2 * D]
        scale = modulation[group, 2 * D:]
        query_heads = split_heads(queries[group])
        key_heads = split_heads(keys[group:].reshape(-1, H * DH))
        value_heads = split_heads(values[group:].reshape(-1, H * DH))
        attended = lax.map(head_attention, (query_heads, key_heads, value_heads))
        attended = attended.transpose(1, 0, 2).reshape(SPAN, H * DH)
        projected = jnp.dot(attended, out_weight, preferred_element_type=jnp.float32)
        stream = hidden[group].astype(jnp.float32) + gate[None, :] * projected
        center = lax.optimization_barrier(jnp.mean(stream, axis=1, keepdims=True))
        spread = lax.optimization_barrier(jnp.mean((stream - center) ** 2, axis=1, keepdims=True))
        normed = (stream - center) / jnp.sqrt(spread + 1e-06) * (1.0 + scale[None, :]) + shift[None, :]
        normed = normed.astype(jnp.bfloat16)
        velocity = jnp.dot(normed, final_weight, preferred_element_type=jnp.float32)
        velocity_list.append(velocity)
        updated_list.append(latents[group] - STRIDE / 1000.0 * velocity)
    velocity_all = jnp.stack(velocity_list)
    next_latents = jnp.concatenate([fresh_noise[None], jnp.stack(updated_list[:-1])], axis=0)
    return (velocity_all, next_latents)
```

```python
import functools
import math

import jax
import jax.numpy as jnp
from jax import lax
from jax.experimental import pallas as pl
from jax.experimental.pallas import tpu as pltpu
from jax.sharding import PartitionSpec as P

D = 3072
H = 16
DH = 128
TEMB = 256
STRIDE = 125
NX, NC, NY, NZ = 4, 2, 4, 8
NQ = NX * NC
TOK = 48
COLS = D // NQ
LAT = 64
SCALE = DH**-0.5 * math.log2(math.e)
MESH = pl.DeviceIdType.MESH


def place(x, c, y, z):
    return {"queue": x * NC + c, "seq": z * NY + y}


def remote(src, dst, send_sem, recv_sem, device):
    return pltpu.make_async_remote_copy(
        src_ref=src,
        dst_ref=dst,
        send_sem=send_sem,
        recv_sem=recv_sem,
        device_id=device,
        device_id_type=MESH,
    )


def wait_bytes(ref, sem):
    pltpu.make_async_copy(ref, ref, sem).wait()


def attend(i, keys, values, q_buf, acc, peak):
    count = keys.shape[0]
    query = q_buf[:, i].reshape(NY * 2 * TOK, DH)
    extended = jnp.concatenate([values, jnp.ones_like(values)], axis=1)
    for part in range(3):
        rows = slice(part * 128, part * 128 + 128)
        scores = (
            lax.dot_general(
                query[rows], keys, (((1,), (1,)), ((), ())), preferred_element_type=jnp.float32
            )
            * SCALE
        )
        old = peak[i, rows, :]
        new = jnp.maximum(old, jnp.max(scores, axis=1, keepdims=True))
        factor = jnp.exp2(old - new)
        weights = jnp.exp2(scores - jnp.concatenate([new] * (count // 128), axis=1))
        mixed = jnp.dot(
            weights.astype(jnp.bfloat16), extended, preferred_element_type=jnp.float32
        )
        acc[i, rows, :] = acc[i, rows, :] * jnp.concatenate([factor, factor], axis=1) + mixed
        peak[i, rows, :] = new


def attend_pair(p, kv, q_buf, acc, peak):
    rows = NZ * TOK

    def both(i, carry):
        keys = kv[pl.ds(2 * p, 2), 0].reshape(2 * rows, DH)
        values = kv[pl.ds(2 * p, 2), 1].reshape(2 * rows, DH)
        attend(i, keys, values, q_buf, acc, peak)
        return carry

    lax.fori_loop(0, 2 * p + 1, both, 0)
    last = 2 * p + 1
    attend(
        last,
        kv[last, 0].reshape(rows, DH),
        kv[last, 1].reshape(rows, DH),
        q_buf,
        acc,
        peak,
    )


def mix_kernel(
    q_ref,
    k_ref,
    v_ref,
    hid_ref,
    act_ref,
    o_all,
    hid_all,
    act_all,
    kv,
    q_buf,
    acc,
    peak,
    o_part,
    o_recv,
    s_part,
    s_recv,
    merged,
    send_a,
    send_h,
    send_x,
    send_y,
    send_o,
    send_z,
    send_g,
    send_c,
    recv_kv,
    recv_q,
    recv_h,
    recv_x,
    recv_xr,
    recv_y,
    recv_yr,
    recv_o,
    recv_s,
    recv_z,
    recv_g,
    recv_gr,
    recv_c,
):
    queue = lax.axis_index("queue")
    seq = lax.axis_index("seq")
    x, c = queue // NC, queue % NC
    z, y = seq // NY, seq % NY
    xl, xr = (x + NX - 1) % NX, (x + 1) % NX
    yl, yr = (y + NY - 1) % NY, (y + 1) % NY
    y2 = (y + 2) % NY
    zk = z // 4
    xt = (z + queue) % NX

    def columns(ref, head):
        return ref.at[:, pl.ds(pl.multiple_of(head * DH, DH), DH)]

    def send_kv(j, carry):
        zt, ct = (z + j // 2) % NZ, (c + j % 2) % NC
        head = 2 * zt + ct
        device = place(x, ct, y, zt)
        remote(
            columns(k_ref, head), kv.at[queue, 0, z], send_a.at[0], recv_kv.at[c], device
        ).start()
        remote(
            columns(v_ref, head), kv.at[queue, 1, z], send_a.at[0], recv_kv.at[c], device
        ).start()
        return carry

    lax.fori_loop(1, 16, send_kv, 0)
    own_head = 2 * z + c
    pltpu.make_async_copy(columns(k_ref, own_head), kv.at[queue, 0, z], recv_kv.at[c]).start()
    pltpu.make_async_copy(columns(v_ref, own_head), kv.at[queue, 1, z], recv_kv.at[c]).start()

    def send_q(j, carry):
        zt, ct = (z + j // 2) % NZ, (c + j % 2) % NC
        remote(
            columns(q_ref, 2 * zt + ct),
            q_buf.at[y, queue, zk],
            send_a.at[1],
            recv_q.at[0],
            place(xt, ct, y, zt),
        ).start()
        return carry

    lax.fori_loop(1, 16, send_q, 0)

    @pl.when(xt != x)
    def _():
        remote(
            columns(q_ref, own_head),
            q_buf.at[y, queue, zk],
            send_a.at[2],
            recv_q.at[0],
            place(xt, c, y, z),
        ).start()

    @pl.when(xt == x)
    def _():
        pltpu.make_async_copy(
            columns(q_ref, own_head), q_buf.at[y, queue, zk], recv_q.at[0]
        ).start()

    def hidden_part(d):
        to = (queue + d) % NQ
        return remote(
            hid_ref.at[:, pl.ds(pl.multiple_of(to * COLS, 128), COLS)],
            hid_all.at[queue],
            send_h.at[0],
            recv_h.at[0],
            {"queue": to, "seq": seq},
        )

    def act_part(d):
        to = (queue + d) % NQ
        return remote(
            act_ref,
            act_all.at[queue],
            send_h.at[1],
            recv_h.at[1],
            {"queue": to, "seq": seq},
        )

    def send_hidden(d, carry):
        hidden_part(d).start()
        act_part(d).start()
        return carry

    lax.fori_loop(1, NQ, send_hidden, 0)
    pltpu.make_async_copy(
        hid_ref.at[:, pl.ds(pl.multiple_of(queue * COLS, 128), COLS)],
        hid_all.at[queue],
        recv_h.at[0],
    ).start()
    pltpu.make_async_copy(act_ref, act_all.at[queue], recv_h.at[1]).start()

    acc[...] = jnp.zeros_like(acc)
    peak[...] = jnp.full_like(peak, -1e30)

    for blk in range(2):
        mine = 2 * x + blk
        wait_bytes(kv.at[mine], recv_kv.at[blk])
        for side, to in ((0, xr), (1, xl)):
            remote(
                kv.at[mine],
                kv.at[mine],
                send_x.at[blk, side],
                recv_x.at[blk, side],
                place(to, c, y, z),
            ).start()

    wait_bytes(q_buf.at[y], recv_q.at[0])
    for side, to in ((0, yr), (1, yl)):
        remote(
            q_buf.at[y], q_buf.at[y], send_y.at[side], recv_y.at[side], place(x, c, to, z)
        ).start()
    wait_bytes(q_buf.at[yl], recv_y.at[0])
    remote(
        q_buf.at[yl, pl.ds(0, 4)],
        q_buf.at[yl, pl.ds(0, 4)],
        send_y.at[2],
        recv_yr.at[0],
        place(x, c, yr, z),
    ).start()
    wait_bytes(q_buf.at[yr], recv_y.at[1])
    remote(
        q_buf.at[yr, pl.ds(4, 4)],
        q_buf.at[yr, pl.ds(4, 4)],
        send_y.at[3],
        recv_yr.at[1],
        place(x, c, yl, z),
    ).start()
    wait_bytes(q_buf.at[y2, pl.ds(0, 4)], recv_yr.at[0])
    wait_bytes(q_buf.at[y2, pl.ds(4, 4)], recv_yr.at[1])

    attend_pair(x, kv, q_buf, acc, peak)

    wait_bytes(kv.at[2 * xl], recv_x.at[0, 0])
    remote(
        kv.at[2 * xl], kv.at[2 * xl], send_x.at[0, 2], recv_xr.at[0], place(xr, c, y, z)
    ).start()
    wait_bytes(kv.at[2 * xl + 1], recv_x.at[1, 0])
    wait_bytes(kv.at[2 * xr + 1], recv_x.at[1, 1])
    remote(
        kv.at[2 * xr + 1], kv.at[2 * xr + 1], send_x.at[1, 2], recv_xr.at[1], place(xl, c, y, z)
    ).start()
    attend_pair(xl, kv, q_buf, acc, peak)
    wait_bytes(kv.at[2 * xr], recv_x.at[0, 1])
    attend_pair(xr, kv, q_buf, acc, peak)
    x2 = (x + 2) % NX
    wait_bytes(kv.at[2 * x2], recv_xr.at[0])
    wait_bytes(kv.at[2 * x2 + 1], recv_xr.at[1])
    attend_pair(x2, kv, q_buf, acc, peak)

    lane = lax.broadcasted_iota(jnp.int32, (2 * TOK, 128), 1)
    row = lax.broadcasted_iota(jnp.int32, (2 * TOK, 128), 0)
    diagonal = lane == row

    def finish(g, carry):
        total = acc[g, :, 128:]
        out = (acc[g, :, :128] / total).astype(jnp.bfloat16)
        level = peak[g] + jnp.log2(total)
        for part in range(NY):
            rows = slice(part * 2 * TOK, (part + 1) * 2 * TOK)
            o_part[part, g] = out[rows].reshape(2, TOK, DH)
            s_part[part, pl.ds(g, 1), :] = jnp.sum(
                jnp.where(diagonal, level[rows], 0.0), axis=0, keepdims=True
            )
        return carry

    lax.fori_loop(0, NQ, finish, 0)

    def partial_copies(d):
        to = (y + d) % NY
        device = place(x, c, to, z)
        return (
            remote(o_part.at[to], o_recv.at[y], send_o.at[d - 1, 0], recv_o.at[d - 1], device),
            remote(s_part.at[to], s_recv.at[y], send_o.at[d - 1, 1], recv_s.at[d - 1], device),
        )

    for d in (2, 1, 3):
        for copy in partial_copies(d):
            copy.start()
    for d in (1, 2, 3):
        source = (y + NY - d) % NY
        wait_bytes(o_recv.at[source], recv_o.at[d - 1])
        wait_bytes(s_recv.at[source], recv_s.at[d - 1])

    def column(vector):
        return jnp.sum(
            jnp.where(diagonal, jnp.broadcast_to(vector, (2 * TOK, 128)), 0.0),
            axis=1,
            keepdims=True,
        )

    def merge(g, carry):
        levels = [column(s_part[y, pl.ds(g, 1), :])]
        outs = [o_part[y, g]]
        for d in (1, 2, 3):
            source = (y + d) % NY
            levels.append(column(s_recv[source, pl.ds(g, 1), :]))
            outs.append(o_recv[source, g])
        top = functools.reduce(jnp.maximum, levels)
        shares = [jnp.exp2(level - top) for level in levels]
        total = functools.reduce(jnp.add, shares)
        mixed = functools.reduce(
            jnp.add,
            [
                share * out.reshape(2 * TOK, DH).astype(jnp.float32)
                for share, out in zip(shares, outs)
            ],
        )
        merged[g] = (mixed / total).astype(jnp.bfloat16).reshape(2, TOK, DH)
        for half in range(2):
            zt = (x + 8 - g) % 4 + 4 * half

            @pl.when(zt != z)
            def _():
                remote(
                    merged.at[g, half],
                    o_all.at[c, g, z],
                    send_z.at[0],
                    recv_z.at[0],
                    place(x, c, y, zt),
                ).start()

            @pl.when(zt == z)
            def _():
                pltpu.make_async_copy(
                    merged.at[g, half], o_all.at[c, g, z], recv_z.at[0]
                ).start()

        return carry

    lax.fori_loop(0, NQ, merge, 0)

    other = place(x, 1 - c, y, z)

    def across(g, slot):
        return remote(o_all.at[c, g], o_all.at[c, g], send_c.at[slot], recv_c.at[slot], other)

    def firsts(xs):
        return (xs + 8 - z) % 4

    mine = firsts(x)
    wait_bytes(o_all.at[c, pl.ds(0, 2)], recv_z.at[0])
    for half in range(2):
        g = mine + 4 * half
        for side, to in ((0, xr), (1, xl)):
            remote(
                o_all.at[c, g],
                o_all.at[c, g],
                send_g.at[half, side],
                recv_g.at[half, side],
                place(to, c, y, z),
            ).start()
    across(mine, 0).start()
    across(mine + 4, 1).start()
    left, right, far = firsts(xl), firsts(xr), firsts(x2)
    wait_bytes(o_all.at[c, left], recv_g.at[0, 0])
    remote(
        o_all.at[c, left], o_all.at[c, left], send_g.at[0, 2], recv_gr.at[0], place(xr, c, y, z)
    ).start()
    across(left, 2).start()
    wait_bytes(o_all.at[c, right + 4], recv_g.at[1, 1])
    remote(
        o_all.at[c, right + 4],
        o_all.at[c, right + 4],
        send_g.at[1, 2],
        recv_gr.at[1],
        place(xl, c, y, z),
    ).start()
    across(right + 4, 3).start()
    wait_bytes(o_all.at[c, left + 4], recv_g.at[1, 0])
    across(left + 4, 4).start()
    wait_bytes(o_all.at[c, right], recv_g.at[0, 1])
    across(right, 5).start()
    wait_bytes(o_all.at[c, far], recv_gr.at[0])
    across(far, 6).start()
    wait_bytes(o_all.at[c, far + 4], recv_gr.at[1])
    across(far + 4, 7).start()

    wait_bytes(hid_all, recv_h.at[0])
    wait_bytes(act_all, recv_h.at[1])
    wait_bytes(hid_all.at[pl.ds(0, 7)], send_h.at[0])
    wait_bytes(act_all.at[pl.ds(0, 7)], send_h.at[1])
    wait_bytes(q_buf.at[pl.ds(0, 3), pl.ds(0, 5)], send_a.at[0])
    wait_bytes(q_buf.at[pl.ds(0, 3), pl.ds(0, 5), 0], send_a.at[1])

    @pl.when(xt != x)
    def _():
        wait_bytes(q_buf.at[0, 0, 0], send_a.at[2])

    for blk in range(2):
        for side in range(3):
            wait_bytes(kv.at[0], send_x.at[blk, side])
            wait_bytes(o_all.at[0, 0], send_g.at[blk, side])
    wait_bytes(q_buf.at[0], send_y.at[0])
    wait_bytes(q_buf.at[0], send_y.at[1])
    wait_bytes(q_buf.at[0, pl.ds(0, 4)], send_y.at[2])
    wait_bytes(q_buf.at[0, pl.ds(0, 4)], send_y.at[3])
    for d in (1, 2, 3):
        for copy in partial_copies(d):
            copy.wait_send()

    wait_bytes(merged.at[pl.ds(0, 7)], send_z.at[0])
    for slot in range(8):
        copy = across(slot, slot)
        copy.wait_send()
        copy.wait_recv()


def mix(queries, keys, values, hidden, activated):
    bf16, f32 = jnp.bfloat16, jnp.float32
    dma = pltpu.SemaphoreType.DMA
    any_spec = pl.BlockSpec(memory_space=pl.ANY)
    return pl.pallas_call(
        mix_kernel,
        out_shape=(
            jax.ShapeDtypeStruct((NC, NQ, NZ, TOK, DH), bf16),
            jax.ShapeDtypeStruct((NQ, TOK, COLS), bf16),
            jax.ShapeDtypeStruct((NQ, 8, TEMB), f32),
        ),
        in_specs=[any_spec] * 5,
        out_specs=(any_spec,) * 3,
        scratch_shapes=[
            pltpu.VMEM((NQ, 2, NZ, TOK, DH), bf16),
            pltpu.VMEM((NY, NQ, 2, TOK, DH), bf16),
            pltpu.VMEM((NQ, NY * 2 * TOK, 256), f32),
            pltpu.VMEM((NQ, NY * 2 * TOK, 128), f32),
            pltpu.VMEM((NY, NQ, 2, TOK, DH), bf16),
            pltpu.VMEM((NY, NQ, 2, TOK, DH), bf16),
            pltpu.VMEM((NY, NQ, 128), f32),
            pltpu.VMEM((NY, NQ, 128), f32),
            pltpu.VMEM((NQ, 2, TOK, DH), bf16),
            dma((3,)),
            dma((2,)),
            dma((2, 3)),
            dma((4,)),
            dma((3, 2)),
            dma((1,)),
            dma((2, 3)),
            dma((8,)),
            dma((2,)),
            dma((1,)),
            dma((2,)),
            dma((2, 2)),
            dma((2,)),
            dma((2,)),
            dma((2,)),
            dma((3,)),
            dma((3,)),
            dma((1,)),
            dma((2, 2)),
            dma((2,)),
            dma((8,)),
        ],
        compiler_params=pltpu.CompilerParams(
            has_side_effects=True, vmem_limit_bytes=40 * 1024 * 1024
        ),
        cost_estimate=pl.CostEstimate(
            flops=3_000_000_000, bytes_accessed=8_000_000, transcendentals=6_000_000
        ),
        name="mix",
    )(queries, keys, values, hidden, activated)


def project_kernel(
    o_ref,
    w_ref,
    hid_ref,
    act_ref,
    mod_ref,
    final_ref,
    lat_ref,
    fresh_ref,
    vel_ref,
    next_ref,
    mod_buf,
    final_buf,
    message,
    received,
    update,
    arrived,
    load_sem,
    send_sem,
    recv_sem,
    move_sem,
):
    queue = lax.axis_index("queue")
    seq = lax.axis_index("seq")
    barrier = pltpu.get_barrier_semaphore()

    def greet(d, carry):
        pl.semaphore_signal(
            barrier,
            inc=1,
            device_id={"queue": (queue + d) % NQ, "seq": seq},
            device_id_type=MESH,
        )
        return carry

    lax.fori_loop(1, NQ, greet, 0)
    loads = [
        pltpu.make_async_copy(
            mod_ref.at[:, pl.ds(pl.multiple_of(part * D + queue * COLS, 128), COLS)],
            mod_buf.at[part],
            load_sem.at[part],
        )
        for part in range(3)
    ]
    loads.append(
        pltpu.make_async_copy(
            final_ref.at[pl.ds(pl.multiple_of(queue * COLS, 128), COLS), :],
            final_buf,
            load_sem.at[3],
        )
    )
    for load in loads:
        load.start()

    projected = None
    for parity in range(NC):
        for zh in range(0, NZ, 2):
            left = jnp.concatenate(
                [o_ref[parity, :, zh + k].reshape(NQ * TOK, DH) for k in range(2)], axis=1
            )
            heads = [2 * (zh + k) + parity for k in range(2)]
            right = jnp.concatenate([w_ref[h * DH : (h + 1) * DH, :] for h in heads], axis=0)
            term = jnp.dot(left, right, preferred_element_type=jnp.float32)
            projected = term if projected is None else projected + term

    for load in loads:
        load.wait()
    act = act_ref[:, 0, :].astype(jnp.bfloat16)
    gate, shift, scale = (
        jnp.dot(act, mod_buf[part], preferred_element_type=jnp.float32) for part in range(3)
    )
    scale = 1.0 + scale
    final = final_buf[...]
    final32 = final.astype(jnp.float32)
    scale_sum = jnp.dot(
        scale, final32, preferred_element_type=jnp.float32, precision=lax.Precision.HIGHEST
    )
    shift_sum = jnp.dot(
        shift, final32, preferred_element_type=jnp.float32, precision=lax.Precision.HIGHEST
    )
    lane = lax.broadcasted_iota(jnp.int32, (TOK, LAT), 1)
    for g in range(NQ):
        rows = slice(g * TOK, (g + 1) * TOK)
        stream = hid_ref[g].astype(jnp.float32) + gate[g : g + 1] * projected[rows]
        center = jnp.mean(stream, axis=1, keepdims=True)
        apart = stream - center
        spread = jnp.sum(apart * apart, axis=1, keepdims=True)
        scaled = (apart * scale[g : g + 1]).astype(jnp.bfloat16)
        message[g, 0:TOK, 0:LAT] = jnp.dot(scaled, final, preferred_element_type=jnp.float32)
        message[g, 0:TOK, LAT:] = jnp.where(
            lane == 0, center, jnp.where(lane == 1, spread, 0.0)
        )
        message[g, TOK : TOK + 8, 0:LAT] = jnp.broadcast_to(scale_sum[g : g + 1], (8, LAT))
        message[g, TOK : TOK + 8, LAT:] = jnp.broadcast_to(shift_sum[g : g + 1], (8, LAT))

    def part(d):
        to = (queue + d) % NQ
        return remote(
            message.at[to],
            received.at[queue],
            send_sem.at[d - 1],
            recv_sem.at[d - 1],
            {"queue": to, "seq": seq},
        )

    pl.semaphore_wait(barrier, NQ - 1)
    for d in range(1, NQ):
        part(d).start()
    blocks = [message[queue]]
    for d in range(1, NQ):
        part(d).wait_recv()
        blocks.append(received[(queue + NQ - d) % NQ])
    centers = [block[0:TOK, LAT : LAT + 1] for block in blocks]
    center = functools.reduce(jnp.add, centers) / NQ
    summed = functools.reduce(jnp.add, [block[0:TOK, LAT + 1 : LAT + 2] for block in blocks])
    mixed = functools.reduce(jnp.add, [block[0:TOK, 0:LAT] for block in blocks])
    offset = functools.reduce(jnp.add, [block[TOK : TOK + 1, LAT:] for block in blocks])
    for block, local in zip(blocks, centers):
        away = local - center
        summed = summed + COLS * (away * away)
        mixed = mixed + away * block[TOK : TOK + 1, 0:LAT]
    velocity = mixed / jnp.sqrt(summed / D + 1e-06) + offset
    vel_ref[...] = velocity
    update[:, 0:LAT] = lat_ref[...] - STRIDE / 1000.0 * velocity
    update[:, LAT:] = jnp.zeros((TOK, LAT), jnp.float32)
    behind = remote(
        update,
        arrived,
        move_sem.at[0],
        move_sem.at[1],
        {"queue": (queue + 1) % NQ, "seq": seq},
    )

    behind.start()
    behind.wait_recv()
    next_ref[...] = jnp.where(queue == 0, fresh_ref[...], arrived[:, 0:LAT])
    behind.wait_send()
    for d in range(1, NQ):
        part(d).wait_send()


def project(o_all, weight, hid_all, act_all, mod_weight, final_weight, latents, fresh):
    f32, bf16 = jnp.float32, jnp.bfloat16
    dma = pltpu.SemaphoreType.DMA
    vmem = pl.BlockSpec(memory_space=pltpu.VMEM)
    any_spec = pl.BlockSpec(memory_space=pl.ANY)
    return pl.pallas_call(
        project_kernel,
        out_shape=(jax.ShapeDtypeStruct((TOK, LAT), f32),) * 2,
        in_specs=[vmem] * 4 + [any_spec] * 2 + [vmem] * 2,
        out_specs=(vmem, vmem),
        scratch_shapes=[
            pltpu.VMEM((3, TEMB, COLS), bf16),
            pltpu.VMEM((COLS, LAT), bf16),
            pltpu.VMEM((NQ, TOK + 8, 128), f32),
            pltpu.VMEM((NQ, TOK + 8, 128), f32),
            pltpu.VMEM((TOK, 128), f32),
            pltpu.VMEM((TOK, 128), f32),
            dma((4,)),
            dma((NQ - 1,)),
            dma((NQ - 1,)),
            dma((2,)),
        ],
        compiler_params=pltpu.CompilerParams(
            collective_id=1, has_side_effects=True, vmem_limit_bytes=40 * 1024 * 1024
        ),
        name="project",
    )(o_all, weight, hid_all, act_all, mod_weight, final_weight, latents, fresh)


def time_embed(step_values):
    halfway = TEMB // 2
    freqs = jnp.exp(-math.log(10000.0) * jnp.arange(halfway, dtype=jnp.float32) / halfway)
    angles = step_values.astype(jnp.float32)[:, None] * freqs[None, :]
    return jnp.concatenate([jnp.cos(angles), jnp.sin(angles)], axis=1)


def body(
    hidden,
    queries,
    keys,
    values,
    timesteps,
    latents,
    fresh_noise,
    out_weight,
    mod_weight,
    final_weight,
):
    queue = lax.axis_index("queue")
    own_columns = lax.dynamic_slice_in_dim(out_weight, queue * COLS, COLS, 1)
    weight = lax.all_gather(own_columns, "seq", axis=0, tiled=True)
    activated = jax.nn.silu(time_embed(timesteps)).astype(jnp.bfloat16).astype(jnp.float32)
    activated = jnp.broadcast_to(activated, (8, TEMB))
    o_all, hid_all, act_all = mix(queries[0], keys[0], values[0], hidden[0], activated)
    velocity, following = project(
        o_all, weight, hid_all, act_all, mod_weight, final_weight, latents[0], fresh_noise
    )
    return velocity[None], following[None]


def solution(mesh):
    placed = (
        P("queue", "seq", None),
        P("queue", "seq", None),
        P("queue", "seq", None),
        P("queue", "seq", None),
        P("queue"),
        P("queue", "seq", None),
        P("seq", None),
        P("seq", None),
        P(),
        P(),
    )
    return jax.shard_map(
        body,
        mesh=mesh,
        in_specs=placed,
        out_specs=(P("queue", "seq", None), P("queue", "seq", None)),
        check_vma=False,
    )
```

```python
import functools
import math

import jax
import jax.numpy as jnp
from jax import lax
from jax.experimental import pallas as pl
from jax.experimental.pallas import tpu as pltpu
from jax.sharding import PartitionSpec as P

D = 3072
H = 16
DH = 128
TEMB = 256
STRIDE = 125
NX, NC, NY, NZ = 4, 2, 4, 8
NQ = NX * NC
TOK = 48
COLS = D // NQ
LAT = 64
ROWS = 2 * TOK
PART = ROWS + 16
SCALE = DH**-0.5 * math.log2(math.e)
MESH = pl.DeviceIdType.MESH


def place(x, c, y, z):
    return {"queue": x * NC + c, "seq": z * NY + y}


def remote(src, dst, send_sem, recv_sem, device):
    return pltpu.make_async_remote_copy(
        src_ref=src,
        dst_ref=dst,
        send_sem=send_sem,
        recv_sem=recv_sem,
        device_id=device,
        device_id_type=MESH,
    )


def wait_bytes(ref, sem):
    pltpu.make_async_copy(ref, ref, sem).wait()


def attend(i, keys, values, q_buf, acc, peak):
    count = keys.shape[0]
    query = q_buf[:, i].reshape(NY * 2 * TOK, DH)
    extended = jnp.concatenate([values, jnp.ones_like(values)], axis=1)
    for part in range(3):
        rows = slice(part * 128, part * 128 + 128)
        scores = (
            lax.dot_general(
                query[rows], keys, (((1,), (1,)), ((), ())), preferred_element_type=jnp.float32
            )
            * SCALE
        )
        old = peak[i, rows, :]
        new = jnp.maximum(old, jnp.max(scores, axis=1, keepdims=True))
        factor = jnp.exp2(old - new)
        weights = jnp.exp2(scores - jnp.concatenate([new] * (count // 128), axis=1))
        mixed = jnp.dot(
            weights.astype(jnp.bfloat16), extended, preferred_element_type=jnp.float32
        )
        acc[i, rows, :] = acc[i, rows, :] * jnp.concatenate([factor, factor], axis=1) + mixed
        peak[i, rows, :] = new


def fused_kernel(
    q_ref,
    k_ref,
    v_ref,
    hid_ref,
    w_ref,
    step_ref,
    mod_ref,
    final_ref,
    lat_ref,
    fresh_ref,
    out_ref,
    kv,
    q_buf,
    acc,
    peak,
    o_part,
    o_recv,
    merged,
    o_all,
    hid_all,
    act_all,
    w_all,
    mod_buf,
    final_buf,
    lat_buf,
    fresh_buf,
    consts,
    sums,
    message,
    received,
    update,
    arrived,
    load_sem,
    send_a,
    send_h,
    send_w_ref,
    send_x,
    send_y,
    send_o,
    send_z,
    send_g,
    send_c,
    send_m,
    recv_kv,
    recv_q,
    recv_h,
    recv_wz,
    recv_wy,
    recv_x,
    recv_xr,
    recv_y,
    recv_o,
    recv_z,
    recv_g,
    recv_c,
    recv_m,
    move_sem,
):
    queue = lax.axis_index("queue")
    seq = lax.axis_index("seq")
    x, c = queue // NC, queue % NC
    z, y = seq // NY, seq % NY
    xl, xr = (x + NX - 1) % NX, (x + 1) % NX
    zk = z // 4
    xt = (z + queue) % NX
    own_head = 2 * z + c
    barrier = pltpu.get_barrier_semaphore()

    def greet(j, carry):
        device = place((x + j // 16) % NX, (c + j % 2) % NC, y, (z + (j // 2) % 8) % NZ)
        pl.semaphore_signal(barrier, inc=1, device_id=device, device_id_type=MESH)
        return carry

    lax.fori_loop(1, 64, greet, 0)
    for d in (1, 2, 3):
        pl.semaphore_signal(
            barrier, inc=1, device_id=place(x, c, (y + d) % NY, z), device_id_type=MESH
        )

    def own_columns(part):
        return pl.ds(pl.multiple_of(part * D + queue * COLS, 128), COLS)

    loads = [
        pltpu.make_async_copy(mod_ref.at[:, own_columns(n)], mod_buf.at[n], load_sem.at[n])
        for n in range(3)
    ]
    loads.append(pltpu.make_async_copy(final_ref.at[:, own_columns(0)], final_buf, load_sem.at[3]))
    loads.append(pltpu.make_async_copy(lat_ref, lat_buf, load_sem.at[4]))
    loads.append(pltpu.make_async_copy(fresh_ref, fresh_buf, load_sem.at[5]))
    for load in loads:
        load.start()

    halfway = TEMB // 2
    index = lax.broadcasted_iota(jnp.int32, (8, halfway), 1).astype(jnp.float32)
    angles = step_ref[0].astype(jnp.float32) * jnp.exp(-math.log(10000.0) * index / halfway)
    embed = jnp.concatenate([jnp.cos(angles), jnp.sin(angles)], axis=1)
    act_all[queue] = embed / (1.0 + jnp.exp(-embed))
    acc[...] = jnp.zeros_like(acc)
    peak[...] = jnp.full_like(peak, -1e30)
    pl.semaphore_wait(barrier, 66)

    def columns(ref, head):
        return ref.at[:, pl.ds(pl.multiple_of(head * DH, DH), DH)]

    def send_q(j, carry):
        zt, ct = (z + j // 2) % NZ, (c + j % 2) % NC
        remote(
            columns(q_ref, 2 * zt + ct),
            q_buf.at[y, queue, zk],
            send_a.at[1],
            recv_q.at[0],
            place(xt, ct, y, zt),
        ).start()
        return carry

    lax.fori_loop(1, 16, send_q, 0)

    @pl.when(xt != x)
    def _():
        remote(
            columns(q_ref, own_head),
            q_buf.at[y, queue, zk],
            send_a.at[2],
            recv_q.at[0],
            place(xt, c, y, z),
        ).start()

    @pl.when(xt == x)
    def _():
        pltpu.make_async_copy(
            columns(q_ref, own_head), q_buf.at[y, queue, zk], recv_q.at[0]
        ).start()

    def send_kv(j, carry):
        zt, ct = (z + j // 2) % NZ, (c + j % 2) % NC
        head = 2 * zt + ct
        device = place(x, ct, y, zt)
        remote(
            columns(k_ref, head), kv.at[queue, 0, z], send_a.at[0], recv_kv.at[c], device
        ).start()
        remote(
            columns(v_ref, head), kv.at[queue, 1, z], send_a.at[0], recv_kv.at[c], device
        ).start()
        return carry

    lax.fori_loop(1, 16, send_kv, 0)
    pltpu.make_async_copy(columns(k_ref, own_head), kv.at[queue, 0, z], recv_kv.at[c]).start()
    pltpu.make_async_copy(columns(v_ref, own_head), kv.at[queue, 1, z], recv_kv.at[c]).start()

    def send_hidden(d, carry):
        to = (queue + d) % NQ
        device = {"queue": to, "seq": seq}
        remote(
            act_all.at[queue], act_all.at[queue], send_h.at[1], recv_h.at[1], device
        ).start()
        remote(
            hid_ref.at[:, pl.ds(pl.multiple_of(to * COLS, 128), COLS)],
            hid_all.at[queue],
            send_h.at[0],
            recv_h.at[0],
            device,
        ).start()
        return carry

    lax.fori_loop(1, NQ, send_hidden, 0)
    pltpu.make_async_copy(hid_ref.at[:, own_columns(0)], hid_all.at[queue], recv_h.at[0]).start()

    wait_bytes(q_buf.at[y], recv_q.at[0])
    for d in (2, 1, 3):
        remote(
            q_buf.at[y],
            q_buf.at[y],
            send_y.at[d - 1],
            recv_y.at[d - 1],
            place(x, c, (y + d) % NY, z),
        ).start()

    for load in loads:
        load.wait()
    wait_bytes(act_all.at[pl.ds(0, NQ - 1)], recv_h.at[1])
    act = act_all[:, 0, :].astype(jnp.bfloat16)
    for n in range(3):
        consts[n] = jnp.dot(act, mod_buf[n], preferred_element_type=jnp.float32)
    consts[2] = 1.0 + consts[2]
    final32 = final_buf[...].astype(jnp.float32)
    for n in range(2):
        sums[n] = lax.dot_general(
            consts[2 - n],
            final32,
            (((1,), (1,)), ((), ())),
            preferred_element_type=jnp.float32,
            precision=lax.Precision.HIGHEST,
        )

    for blk in range(2):
        wait_bytes(kv.at[2 * x + blk], recv_kv.at[blk])
    for k in range(2):
        for side, to in ((0, xr), (1, xl)):
            blk = k if side == 0 else 1 - k
            remote(
                kv.at[2 * x + blk],
                kv.at[2 * x + blk],
                send_x.at[blk, side],
                recv_x.at[blk, side],
                place(to, c, y, z),
            ).start()

    def send_w(d, carry):
        remote(
            w_ref.at[:, own_columns(0)],
            w_all.at[z, y],
            send_w_ref.at[0],
            recv_wz.at[0],
            place(x, c, y, (z + d) % NZ),
        ).start()
        return carry

    lax.fori_loop(1, NZ, send_w, 0)
    pltpu.make_async_copy(w_ref.at[:, own_columns(0)], w_all.at[z, y], recv_wz.at[0]).start()

    for d in (1, 3, 2):
        wait_bytes(q_buf.at[(y + NY - d) % NY], recv_y.at[d - 1])

    lane = lax.broadcasted_iota(jnp.int32, (ROWS, 128), 1)
    row = lax.broadcasted_iota(jnp.int32, (ROWS, 128), 0)
    diagonal = lane == row
    stat_row = lax.broadcasted_iota(jnp.int32, (16, 128), 0)

    def finish(g, carry):
        total = acc[g, :, 128:]
        out = (acc[g, :, :128] / total).astype(jnp.bfloat16)
        level = peak[g] + jnp.log2(total)
        for part in range(NY):
            rows = slice(part * ROWS, (part + 1) * ROWS)
            vector = jnp.sum(jnp.where(diagonal, level[rows], 0.0), axis=0, keepdims=True)
            high = vector.astype(jnp.bfloat16).astype(jnp.float32)
            middle = (vector - high).astype(jnp.bfloat16).astype(jnp.float32)
            low = vector - high - middle
            stats = jnp.where(
                stat_row == 0,
                high,
                jnp.where(stat_row == 1, middle, jnp.where(stat_row == 2, low, 0.0)),
            )
            o_part[part, g, 0:ROWS] = out[rows]
            o_part[part, g, ROWS:] = stats.astype(jnp.bfloat16)
        return carry

    def partial_copy(half, d):
        to = (y + d) % NY
        rows = pl.ds(4 * half, 4)
        return remote(
            o_part.at[to, rows],
            o_recv.at[y, rows],
            send_o.at[half, d - 1],
            recv_o.at[half, d - 1],
            place(x, c, to, z),
        )

    key_rows = NZ * TOK

    def stage(st, carry):
        p = (x + st + st // 2 - 2 * (st // 3)) % NX

        @pl.when(st == 1)
        def _():
            wait_bytes(kv.at[2 * xl], recv_x.at[0, 0])
            remote(
                kv.at[2 * xl], kv.at[2 * xl], send_x.at[0, 2], recv_xr.at[0], place(xr, c, y, z)
            ).start()
            right = 2 * xr + 1
            wait_bytes(kv.at[right], recv_x.at[1, 1])
            remote(
                kv.at[right], kv.at[right], send_x.at[1, 2], recv_xr.at[1], place(xl, c, y, z)
            ).start()
            wait_bytes(kv.at[2 * xr], recv_x.at[0, 1])

        @pl.when(st == 2)
        def _():
            wait_bytes(w_all.at[:, y], recv_wz.at[0])
            for d in (1, 3, 2):
                remote(
                    w_all.at[:, y],
                    w_all.at[:, y],
                    send_w_ref.at[d],
                    recv_wy.at[d - 1],
                    place(x, c, (y + d) % NY, z),
                ).start()
            wait_bytes(kv.at[2 * xl + 1], recv_x.at[1, 0])

        @pl.when(st == 3)
        def _():
            wait_bytes(kv.at[2 * p], recv_xr.at[0])
            wait_bytes(kv.at[2 * p + 1], recv_xr.at[1])

        high, odd = p // 2, p % 2

        def both(i, carry):
            keys = kv[pl.ds(2 * p, 2), 0].reshape(2 * key_rows, DH)
            values = kv[pl.ds(2 * p, 2), 1].reshape(2 * key_rows, DH)
            attend(i, keys, values, q_buf, acc, peak)
            return carry

        def halves(half, carry):
            same = 1 - (high - half) * (high - half)
            count = 4 * high * (1 - half) + (2 * odd + 1) * same
            lax.fori_loop(4 * half, 4 * half + count, both, 0)

            @pl.when(high == half)
            def _():
                last = 2 * p + 1
                attend(
                    last,
                    kv[last, 0].reshape(key_rows, DH),
                    kv[last, 1].reshape(key_rows, DH),
                    q_buf,
                    acc,
                    peak,
                )

            @pl.when(st == 3)
            def _():
                lax.fori_loop(4 * half, 4 * half + 4, finish, 0)
                for d in (2, 1, 3):
                    partial_copy(half, d).start()

            return carry

        return lax.fori_loop(0, 2, halves, carry)

    lax.fori_loop(0, 4, stage, 0)

    def column(stats):
        stats = stats.astype(jnp.float32)
        vector = stats[0:1] + stats[1:2] + stats[2:3]
        return jnp.sum(
            jnp.where(diagonal, jnp.broadcast_to(vector, (ROWS, 128)), 0.0),
            axis=1,
            keepdims=True,
        )

    def merge(g, carry):
        parts = [o_part[y, g]] + [o_recv[(y + d) % NY, g] for d in (1, 2, 3)]
        levels = [column(part[ROWS:]) for part in parts]
        top = functools.reduce(jnp.maximum, levels)
        shares = [jnp.exp2(level - top) for level in levels]
        total = functools.reduce(jnp.add, shares)
        mixed = functools.reduce(
            jnp.add,
            [share * part[:ROWS].astype(jnp.float32) for share, part in zip(shares, parts)],
        )
        merged[g] = (mixed / total).astype(jnp.bfloat16).reshape(2, TOK, DH)
        for k in range(2):
            zt = (x + 8 - g) % 4 + 4 * k

            @pl.when(zt != z)
            def _():
                remote(
                    merged.at[g, k],
                    o_all.at[c, g, z],
                    send_z.at[0],
                    recv_z.at[g // 4],
                    place(x, c, y, zt),
                ).start()

            @pl.when(zt == z)
            def _():
                pltpu.make_async_copy(
                    merged.at[g, k], o_all.at[c, g, z], recv_z.at[g // 4]
                ).start()

        return carry

    def first(xs):
        return (xs + 8 - z) % 4

    def across(g, slot):
        return remote(
            o_all.at[c, g],
            o_all.at[c, g],
            send_c.at[slot],
            recv_c.at[slot],
            place(x, 1 - c, y, z),
        )

    for half in range(2):
        for d in (1, 3, 2):
            wait_bytes(
                o_recv.at[(y + NY - d) % NY, pl.ds(4 * half, 4)], recv_o.at[half, d - 1]
            )
        lax.fori_loop(4 * half, 4 * half + 4, merge, 0)
        g = first(x) + 4 * half
        wait_bytes(o_all.at[c, g], recv_z.at[half])
        for d in (2, 1, 3):
            remote(
                o_all.at[c, g],
                o_all.at[c, g],
                send_g.at[half, d - 1],
                recv_g.at[half, d - 1],
                place((x + d) % NX, c, y, z),
            ).start()
        across(g, 4 * half).start()

    wait_bytes(hid_all, recv_h.at[0])
    for d in (1, 2, 3):
        wait_bytes(w_all.at[:, (y + NY - d) % NY], recv_wy.at[d - 1])

    lat_lane = lax.broadcasted_iota(jnp.int32, (TOK, LAT), 1)
    for half in range(2):
        for d in (1, 3, 2):
            g = first((x + NX - d) % NX) + 4 * half
            wait_bytes(o_all.at[c, g], recv_g.at[half, d - 1])
            across(g, 4 * half + d).start()
        for d in range(NX):
            g = first((x + NX - d) % NX) + 4 * half
            wait_bytes(o_all.at[1 - c, g], recv_c.at[4 * half + d])

        projected = None
        for parity in range(NC):
            for zh in range(0, NZ, 2):
                left = jnp.concatenate(
                    [
                        o_all[parity, 4 * half : 4 * half + 4, zh + k].reshape(4 * TOK, DH)
                        for k in range(2)
                    ],
                    axis=1,
                )
                right = jnp.concatenate(
                    [w_all[zh + k, 2 * parity + n] for k in range(2) for n in range(2)], axis=0
                )
                term = jnp.dot(left, right, preferred_element_type=jnp.float32)
                projected = term if projected is None else projected + term

        for g in range(4 * half, 4 * half + 4):
            rows = slice((g % 4) * TOK, (g % 4 + 1) * TOK)
            stream = hid_all[g].astype(jnp.float32) + consts[0, g : g + 1, :] * projected[rows]
            center = jnp.mean(stream, axis=1, keepdims=True)
            apart = stream - center
            spread = jnp.sum(apart * apart, axis=1, keepdims=True)
            scaled = (apart * consts[2, g : g + 1, :]).astype(jnp.bfloat16)
            message[g, 0:TOK, 0:LAT] = lax.dot_general(
                scaled,
                final_buf[...],
                (((1,), (1,)), ((), ())),
                preferred_element_type=jnp.float32,
            )
            message[g, 0:TOK, LAT:] = jnp.where(
                lat_lane == 0, center, jnp.where(lat_lane == 1, spread, 0.0)
            )
            message[g, TOK:, 0:LAT] = jnp.broadcast_to(sums[0, g : g + 1, :], (8, LAT))
            message[g, TOK:, LAT:] = jnp.broadcast_to(sums[1, g : g + 1, :], (8, LAT))

            @pl.when(queue != g)
            def _():
                remote(
                    message.at[g],
                    received.at[queue],
                    send_m.at[g],
                    recv_m.at[queue],
                    {"queue": g, "seq": seq},
                ).start()

    blocks = [message[queue]]
    for d in range(1, NQ):
        source = (queue + NQ - d) % NQ
        wait_bytes(received.at[source], recv_m.at[source])
        blocks.append(received[source])
    centers = [block[0:TOK, LAT : LAT + 1] for block in blocks]
    center = functools.reduce(jnp.add, centers) / NQ
    summed = functools.reduce(jnp.add, [block[0:TOK, LAT + 1 : LAT + 2] for block in blocks])
    mixed = functools.reduce(jnp.add, [block[0:TOK, 0:LAT] for block in blocks])
    offset = functools.reduce(jnp.add, [block[TOK : TOK + 1, LAT:] for block in blocks])
    for block, local in zip(blocks, centers):
        away = local - center
        summed = summed + COLS * (away * away)
        mixed = mixed + away * block[TOK : TOK + 1, 0:LAT]
    velocity = mixed / jnp.sqrt(summed / D + 1e-06) + offset
    update[:, 0:LAT] = lat_buf[...] - STRIDE / 1000.0 * velocity
    update[:, LAT:] = velocity
    behind = remote(
        update,
        arrived,
        move_sem.at[0],
        move_sem.at[1],
        {"queue": (queue + 1) % NQ, "seq": seq},
    )
    behind.start()
    out_ref[:, 0:LAT] = velocity

    wait_bytes(hid_all.at[pl.ds(0, NQ - 1)], send_h.at[0])
    wait_bytes(act_all.at[pl.ds(0, NQ - 1)], send_h.at[1])
    wait_bytes(q_buf.at[pl.ds(0, 3), pl.ds(0, 5)], send_a.at[0])
    wait_bytes(q_buf.at[pl.ds(0, 3), pl.ds(0, 5), 0], send_a.at[1])

    @pl.when(xt != x)
    def _():
        wait_bytes(q_buf.at[0, 0, 0], send_a.at[2])

    wait_bytes(w_all.at[pl.ds(0, NZ - 1), 0], send_w_ref.at[0])
    for blk in range(2):
        for side in range(3):
            wait_bytes(kv.at[0], send_x.at[blk, side])
    for d in (1, 2, 3):
        wait_bytes(q_buf.at[0], send_y.at[d - 1])
        wait_bytes(w_all.at[:, 0], send_w_ref.at[d])
        for half in range(2):
            wait_bytes(o_part.at[0, pl.ds(0, 4)], send_o.at[half, d - 1])
            wait_bytes(o_all.at[0, 0], send_g.at[half, d - 1])
    wait_bytes(merged.at[pl.ds(0, 7)], send_z.at[0])
    for slot in range(8):
        wait_bytes(o_all.at[0, 0], send_c.at[slot])
    for g in range(NQ):

        @pl.when(queue != g)
        def _():
            wait_bytes(message.at[0], send_m.at[g])

    behind.wait_recv()
    out_ref[:, LAT:] = jnp.where(queue == 0, fresh_buf[...], arrived[:, 0:LAT])
    behind.wait_send()


def fused(*operands):
    bf16, f32 = jnp.bfloat16, jnp.float32
    vmem, dma = pltpu.VMEM, pltpu.SemaphoreType.DMA
    in_specs = [pl.BlockSpec(memory_space=pl.ANY)] * 10
    in_specs[5] = pl.BlockSpec(memory_space=pltpu.SMEM)
    return pl.pallas_call(
        fused_kernel,
        out_shape=jax.ShapeDtypeStruct((TOK, 2 * LAT), f32),
        in_specs=in_specs,
        out_specs=pl.BlockSpec(memory_space=pltpu.VMEM),
        scratch_shapes=[
            vmem((NQ, 2, NZ, TOK, DH), bf16),
            vmem((NY, NQ, 2, TOK, DH), bf16),
            vmem((NQ, NY * ROWS, 256), f32),
            vmem((NQ, NY * ROWS, 128), f32),
            vmem((NY, NQ, PART, DH), bf16),
            vmem((NY, NQ, PART, DH), bf16),
            vmem((NQ, 2, TOK, DH), bf16),
            vmem((NC, NQ, NZ, TOK, DH), bf16),
            vmem((NQ, TOK, COLS), bf16),
            vmem((NQ, 8, TEMB), f32),
            vmem((NZ, NY, 64, COLS), bf16),
            vmem((3, TEMB, COLS), bf16),
            vmem((LAT, COLS), bf16),
            vmem((TOK, LAT), f32),
            vmem((TOK, LAT), f32),
            vmem((3, NQ, COLS), f32),
            vmem((2, NQ, LAT), f32),
            vmem((NQ, TOK + 8, 128), f32),
            vmem((NQ, TOK + 8, 128), f32),
            vmem((TOK, 128), f32),
            vmem((TOK, 128), f32),
            dma((6,)),
            dma((3,)),
            dma((2,)),
            dma((4,)),
            dma((2, 3)),
            dma((3,)),
            dma((2, 3)),
            dma((1,)),
            dma((2, 3)),
            dma((8,)),
            dma((NQ,)),
            dma((2,)),
            dma((1,)),
            dma((2,)),
            dma((1,)),
            dma((3,)),
            dma((2, 2)),
            dma((2,)),
            dma((3,)),
            dma((2, 3)),
            dma((2,)),
            dma((2, 3)),
            dma((8,)),
            dma((NQ,)),
            dma((2,)),
        ],
        compiler_params=pltpu.CompilerParams(
            collective_id=0, has_side_effects=True, vmem_limit_bytes=60 * 1024 * 1024
        ),
        name="fused",
    )(*operands)


def body(
    hidden,
    queries,
    keys,
    values,
    timesteps,
    latents,
    fresh_noise,
    out_weight,
    mod_weight,
    final_weight,
):
    result = fused(
        queries[0],
        keys[0],
        values[0],
        hidden[0],
        out_weight,
        timesteps,
        mod_weight,
        final_weight.T,
        latents[0],
        fresh_noise,
    )
    return result[None, :, :LAT], result[None, :, LAT:]


def solution(mesh):
    placed = (
        P("queue", "seq", None),
        P("queue", "seq", None),
        P("queue", "seq", None),
        P("queue", "seq", None),
        P("queue"),
        P("queue", "seq", None),
        P("seq", None),
        P("seq", None),
        P(),
        P(),
    )
    return jax.shard_map(
        body,
        mesh=mesh,
        in_specs=placed,
        out_specs=(P("queue", "seq", None), P("queue", "seq", None)),
        check_vma=False,
    )
```

```python
import functools
import math

import jax
import jax.numpy as jnp
from jax import lax
from jax.experimental import pallas as pl
from jax.experimental.pallas import tpu as pltpu
from jax.sharding import PartitionSpec as P

D = 3072
H = 16
DH = 128
TEMB = 256
STRIDE = 125
NX, NC, NY, NZ = 4, 2, 4, 8
NQ = NX * NC
TOK = 48
COLS = D // NQ
LAT = 64
ROWS = 2 * TOK
PART = 4 * ROWS + 16
MSG = TOK // 2 + 8
SCALE = DH**-0.5 * math.log2(math.e)
MESH = pl.DeviceIdType.MESH


def place(x, c, y, z):
    return {"queue": x * NC + c, "seq": z * NY + y}


def remote(src, dst, send_sem, recv_sem, device):
    return pltpu.make_async_remote_copy(
        src_ref=src,
        dst_ref=dst,
        send_sem=send_sem,
        recv_sem=recv_sem,
        device_id=device,
        device_id_type=MESH,
    )


def wait_bytes(ref, sem):
    pltpu.make_async_copy(ref, ref, sem).wait()


def attend(i, keys, values, q_buf, acc, peak):
    count = keys.shape[0]
    query = q_buf[:, i].reshape(NY * 2 * TOK, DH)
    extended = jnp.concatenate([values, jnp.ones_like(values)], axis=1)
    for part in range(3):
        rows = slice(part * 128, part * 128 + 128)
        scores = (
            lax.dot_general(
                query[rows], keys, (((1,), (1,)), ((), ())), preferred_element_type=jnp.float32
            )
            * SCALE
        )
        old = peak[i, rows, :]
        new = jnp.maximum(old, jnp.max(scores, axis=1, keepdims=True))
        factor = jnp.exp2(old - new)
        weights = jnp.exp2(scores - jnp.concatenate([new] * (count // 128), axis=1))
        mixed = jnp.dot(
            weights.astype(jnp.bfloat16), extended, preferred_element_type=jnp.float32
        )
        acc[i, rows, :] = acc[i, rows, :] * jnp.concatenate([factor, factor], axis=1) + mixed
        peak[i, rows, :] = new


def fused_kernel(
    q_ref,
    k_ref,
    v_ref,
    hid_ref,
    w_ref,
    step_ref,
    mod_ref,
    final_ref,
    lat_ref,
    fresh_ref,
    out_ref,
    k_buf,
    v_buf,
    q_buf,
    acc,
    peak,
    o_part,
    o_recv,
    merged,
    o_all,
    hid_all,
    act_all,
    w_all,
    mod_buf,
    final_buf,
    lat_behind,
    fresh_buf,
    consts,
    sums,
    message,
    received,
    load_sem,
    send_a,
    send_h,
    send_wy,
    send_wz,
    send_x,
    send_y,
    send_o,
    send_z,
    send_g,
    send_c,
    send_m,
    recv_k,
    recv_v,
    recv_q,
    recv_h,
    recv_wy,
    recv_wz,
    recv_x,
    recv_y,
    recv_o,
    recv_z,
    recv_g,
    recv_c,
    recv_m,
):
    queue = lax.axis_index("queue")
    seq = lax.axis_index("seq")
    x, c = queue // NC, queue % NC
    z, y = seq // NY, seq % NY
    xl, xr, x2 = (x + NX - 1) % NX, (x + 1) % NX, (x + 2) % NX
    yl, yr, y2 = (y + NY - 1) % NY, (y + 1) % NY, (y + 2) % NY
    zl, zr = (z + NZ - 1) % NZ, (z + 1) % NZ
    zk = z // 4
    xt = (z + queue) % NX
    own_head = 2 * z + c
    barrier = pltpu.get_barrier_semaphore()

    def greet(j, carry):
        device = place((x + j // 16) % NX, (c + j % 2) % NC, y, (z + (j // 2) % 8) % NZ)
        pl.semaphore_signal(barrier, inc=1, device_id=device, device_id_type=MESH)
        return carry

    lax.fori_loop(1, 64, greet, 0)
    for d in (1, 2, 3):
        pl.semaphore_signal(
            barrier, inc=1, device_id=place(x, c, (y + d) % NY, z), device_id_type=MESH
        )

    def own_columns(part):
        return pl.ds(pl.multiple_of(part * D + queue * COLS, 128), COLS)

    loads = [
        pltpu.make_async_copy(mod_ref.at[:, own_columns(n)], mod_buf.at[n], load_sem.at[n])
        for n in range(3)
    ]
    loads.append(pltpu.make_async_copy(final_ref.at[:, own_columns(0)], final_buf, load_sem.at[3]))
    loads.append(pltpu.make_async_copy(fresh_ref, fresh_buf, load_sem.at[4]))
    for load in loads:
        load.start()

    pl.semaphore_wait(barrier, 66)

    def columns(ref, head):
        return ref.at[:, pl.ds(pl.multiple_of(head * DH, DH), DH)]

    def by_head(array, ref, target, sem, xs):
        def send(j, carry):
            zt, ct = (z + j // 2) % NZ, (c + j % 2) % NC
            remote(
                columns(ref, 2 * zt + ct), target, send_a.at[array], sem, place(xs, ct, y, zt)
            ).start()
            return carry

        lax.fori_loop(1, 16, send, 0)

    by_head(0, k_ref, k_buf.at[queue, z], recv_k.at[c], x)
    pltpu.make_async_copy(columns(k_ref, own_head), k_buf.at[queue, z], recv_k.at[c]).start()
    by_head(1, q_ref, q_buf.at[y, queue, zk], recv_q.at[0], xt)

    @pl.when(xt != x)
    def _():
        remote(
            columns(q_ref, own_head),
            q_buf.at[y, queue, zk],
            send_a.at[3],
            recv_q.at[0],
            place(xt, c, y, z),
        ).start()

    @pl.when(xt == x)
    def _():
        pltpu.make_async_copy(
            columns(q_ref, own_head), q_buf.at[y, queue, zk], recv_q.at[0]
        ).start()

    by_head(2, v_ref, v_buf.at[queue, z], recv_v.at[c], x)
    pltpu.make_async_copy(columns(v_ref, own_head), v_buf.at[queue, z], recv_v.at[c]).start()

    for d in (1, 2, 3):
        remote(
            w_ref.at[:, own_columns(0)],
            w_all.at[z, y],
            send_wy.at[d - 1],
            recv_wy.at[0],
            place(x, c, (y + d) % NY, z),
        ).start()
    pltpu.make_async_copy(w_ref.at[:, own_columns(0)], w_all.at[z, y], recv_wy.at[0]).start()

    halfway = TEMB // 2
    index = lax.broadcasted_iota(jnp.int32, (8, halfway), 1).astype(jnp.float32)
    angles = step_ref[0].astype(jnp.float32) * jnp.exp(-math.log(10000.0) * index / halfway)
    embed = jnp.concatenate([jnp.cos(angles), jnp.sin(angles)], axis=1)
    act_all[queue] = embed / (1.0 + jnp.exp(-embed))

    def send_hidden(d, carry):
        to = (queue + d) % NQ
        device = {"queue": to, "seq": seq}
        remote(
            act_all.at[queue], act_all.at[queue], send_h.at[1], recv_h.at[1], device
        ).start()
        remote(
            hid_ref.at[:, pl.ds(pl.multiple_of(to * COLS, 128), COLS)],
            hid_all.at[queue],
            send_h.at[0],
            recv_h.at[0],
            device,
        ).start()
        return carry

    lax.fori_loop(1, NQ, send_hidden, 0)
    pltpu.make_async_copy(hid_ref.at[:, own_columns(0)], hid_all.at[queue], recv_h.at[0]).start()

    @pl.when(queue < NQ - 1)
    def _():
        remote(
            lat_ref,
            lat_behind,
            send_h.at[2],
            recv_h.at[2],
            {"queue": (queue + 1) % NQ, "seq": seq},
        ).start()

    acc[...] = jnp.zeros_like(acc)
    peak[...] = jnp.full_like(peak, -1e30)

    def along_x(array, ref):
        for n in range(2):
            for side, to in ((0, xr), (1, xl)):
                blk = n if side == 0 else 1 - n
                block = ref.at[2 * x + blk]
                remote(
                    block,
                    block,
                    send_x.at[array, side, blk],
                    recv_x.at[array, side, blk],
                    place(to, c, y, z),
                ).start()

    def relay_x(array, ref):
        for side, source, to in ((0, xl, xr), (1, xr, xl)):
            block = ref.at[2 * source + side]
            wait_bytes(block, recv_x.at[array, side, side])
            remote(
                block,
                block,
                send_x.at[array, side, 2],
                recv_x.at[array, side, 2],
                place(to, c, y, z),
            ).start()

    for blk in range(2):
        wait_bytes(k_buf.at[2 * x + blk], recv_k.at[blk])
    along_x(0, k_buf)

    wait_bytes(q_buf.at[y], recv_q.at[0])
    for side, to in ((0, yr), (1, yl)):
        remote(
            q_buf.at[y], q_buf.at[y], send_y.at[side, 0], recv_y.at[side, 0], place(x, c, to, z)
        ).start()

    for load in loads:
        load.wait()
    wait_bytes(act_all.at[pl.ds(0, NQ - 1)], recv_h.at[1])
    act = act_all[:, 0, :].astype(jnp.bfloat16)
    for n in range(3):
        consts[n] = jnp.dot(act, mod_buf[n], preferred_element_type=jnp.float32)
    consts[2] = 1.0 + consts[2]
    final32 = final_buf[...].astype(jnp.float32)
    for n in range(2):
        sums[n] = lax.dot_general(
            consts[2 - n],
            final32,
            (((1,), (1,)), ((), ())),
            preferred_element_type=jnp.float32,
            precision=lax.Precision.HIGHEST,
        )

    relay_x(0, k_buf)
    for blk in range(2):
        wait_bytes(v_buf.at[2 * x + blk], recv_v.at[blk])
    along_x(1, v_buf)
    for side, source, to in ((0, yl, yr), (1, yr, yl)):
        wait_bytes(q_buf.at[source], recv_y.at[side, 0])
        slab = q_buf.at[source, pl.ds(4 * side, 4)]
        remote(
            slab, slab, send_y.at[side, 1], recv_y.at[side, 1], place(x, c, to, z)
        ).start()

    def ring_z(step):
        for side, to in ((0, zr), (1, zl)):
            back = NZ - step if side == 0 else step
            rows = pl.ds(0, NY) if step < 3 else pl.ds(2 * side, 2)
            chunk = w_all.at[(z + back) % NZ]
            if step:
                wait_bytes(chunk, recv_wz.at[side, step - 1])
            chunk = w_all.at[(z + back) % NZ, rows]
            remote(
                chunk,
                chunk,
                send_wz.at[side, step],
                recv_wz.at[side, step],
                place(x, c, y, to),
            ).start()

    wait_bytes(w_all.at[z], recv_wy.at[0])
    ring_z(0)
    for side in range(2):
        wait_bytes(q_buf.at[y2, pl.ds(4 * side, 4)], recv_y.at[side, 1])

    lane = lax.broadcasted_iota(jnp.int32, (ROWS, 128), 1)
    row = lax.broadcasted_iota(jnp.int32, (ROWS, 128), 0)
    diagonal = lane == row
    stat_row = lax.broadcasted_iota(jnp.int32, (16, 128), 0)

    def finish(half):
        vectors = [[] for _ in range(NY)]
        for k in range(4):
            g = 4 * half + k
            total = acc[g, :, 128:]
            out = (acc[g, :, :128] / total).astype(jnp.bfloat16)
            level = peak[g] + jnp.log2(total)
            for part in range(NY):
                rows = slice(part * ROWS, (part + 1) * ROWS)
                vector = jnp.sum(jnp.where(diagonal, level[rows], 0.0), axis=0, keepdims=True)
                high = vector.astype(jnp.bfloat16).astype(jnp.float32)
                middle = (vector - high).astype(jnp.bfloat16).astype(jnp.float32)
                vectors[part] += [high, middle, vector - high - middle]
                o_part[part, half, k * ROWS : (k + 1) * ROWS] = out[rows]
        for part in range(NY):
            stats = jnp.zeros((16, 128), jnp.float32)
            for n, vector in enumerate(vectors[part]):
                stats = jnp.where(stat_row == n, vector, stats)
            o_part[part, half, 4 * ROWS :] = stats.astype(jnp.bfloat16)

    def partial_copy(half, d):
        to = (y + d) % NY
        return remote(
            o_part.at[to, half],
            o_recv.at[y, half],
            send_o.at[half, d - 1],
            recv_o.at[half, d - 1],
            place(x, c, to, z),
        )

    key_rows = NZ * TOK

    def stage(st, carry):
        p = (x + st + st // 2 - 2 * (st // 3)) % NX

        @pl.when(st == 1)
        def _():
            relay_x(1, v_buf)
            for ref, array in ((k_buf, 0), (v_buf, 1)):
                wait_bytes(ref.at[2 * xr], recv_x.at[array, 1, 0])

        @pl.when(st == 2)
        def _():
            ring_z(1)
            for ref, array in ((k_buf, 0), (v_buf, 1)):
                wait_bytes(ref.at[2 * xl + 1], recv_x.at[array, 0, 1])

        @pl.when(st == 3)
        def _():
            for ref, array in ((k_buf, 0), (v_buf, 1)):
                for side in range(2):
                    wait_bytes(ref.at[2 * x2 + side], recv_x.at[array, side, 2])

        high, odd = p // 2, p % 2

        def both(i, carry):
            keys = k_buf[pl.ds(2 * p, 2)].reshape(2 * key_rows, DH)
            values = v_buf[pl.ds(2 * p, 2)].reshape(2 * key_rows, DH)
            attend(i, keys, values, q_buf, acc, peak)
            return carry

        def halves(half, carry):
            same = 1 - (high - half) * (high - half)
            count = 4 * high * (1 - half) + (2 * odd + 1) * same
            lax.fori_loop(4 * half, 4 * half + count, both, 0)

            @pl.when(high == half)
            def _():
                last = 2 * p + 1
                attend(
                    last,
                    k_buf[last].reshape(key_rows, DH),
                    v_buf[last].reshape(key_rows, DH),
                    q_buf,
                    acc,
                    peak,
                )

            @pl.when(st == 3)
            def _():
                finish(half)
                for d in (2, 1, 3):
                    partial_copy(half, d).start()

            return carry

        return lax.fori_loop(0, 2, halves, carry)

    lax.fori_loop(0, 4, stage, 0)
    ring_z(2)

    def column(vector):
        return jnp.sum(
            jnp.where(diagonal, jnp.broadcast_to(vector, (ROWS, 128)), 0.0),
            axis=1,
            keepdims=True,
        )

    def merge(half):
        refs = [o_part.at[y, half]] + [o_recv.at[(y + d) % NY, half] for d in (1, 2, 3)]
        stats = [ref[4 * ROWS :].astype(jnp.float32) for ref in refs]
        for k in range(4):
            g = 4 * half + k
            levels = [
                column(stat[3 * k : 3 * k + 1] + stat[3 * k + 1 : 3 * k + 2] + stat[3 * k + 2 : 3 * k + 3])
                for stat in stats
            ]
            top = functools.reduce(jnp.maximum, levels)
            shares = [jnp.exp2(level - top) for level in levels]
            total = functools.reduce(jnp.add, shares)
            mixed = functools.reduce(
                jnp.add,
                [
                    share * ref[k * ROWS : (k + 1) * ROWS].astype(jnp.float32)
                    for share, ref in zip(shares, refs)
                ],
            )
            merged[g] = (mixed / total).astype(jnp.bfloat16).reshape(2, TOK, DH)
            for n in range(2):
                zt = (x + 8 - g) % 4 + 4 * n

                @pl.when(zt != z)
                def _():
                    remote(
                        merged.at[g, n],
                        o_all.at[c, g, z],
                        send_z.at[0],
                        recv_z.at[half],
                        place(x, c, y, zt),
                    ).start()

                @pl.when(zt == z)
                def _():
                    pltpu.make_async_copy(
                        merged.at[g, n], o_all.at[c, g, z], recv_z.at[half]
                    ).start()

    def first(xs):
        return (xs + 8 - z) % 4

    def across(g, slot):
        return remote(
            o_all.at[c, g],
            o_all.at[c, g],
            send_c.at[slot],
            recv_c.at[slot],
            place(x, 1 - c, y, z),
        )

    for half in range(2):
        for d in (1, 3, 2):
            wait_bytes(o_recv.at[(y + NY - d) % NY, half], recv_o.at[half, d - 1])
        merge(half)
        g = first(x) + 4 * half
        wait_bytes(o_all.at[c, g], recv_z.at[half])
        for d in (2, 1, 3):
            remote(
                o_all.at[c, g],
                o_all.at[c, g],
                send_g.at[half, d - 1],
                recv_g.at[half, d - 1],
                place((x + d) % NX, c, y, z),
            ).start()
        across(g, 4 * half).start()
        if half == 0:
            ring_z(3)

    wait_bytes(hid_all, recv_h.at[0])
    for side in range(2):
        wait_bytes(w_all.at[(z + 4) % NZ, pl.ds(2 * side, 2)], recv_wz.at[side, 3])

    token_lane = lax.broadcasted_iota(jnp.int32, (TOK, 128), 1)
    token_row = lax.broadcasted_iota(jnp.int32, (TOK, 128), 0)
    token_diagonal = token_lane == token_row
    last_row = lax.broadcasted_iota(jnp.int32, (8, 128), 0)

    def as_row(vector):
        return jnp.sum(
            jnp.where(token_diagonal, jnp.broadcast_to(vector, (TOK, 128)), 0.0),
            axis=0,
            keepdims=True,
        )

    def as_column(vector):
        return jnp.sum(
            jnp.where(token_diagonal, jnp.broadcast_to(vector, (TOK, 128)), 0.0),
            axis=1,
            keepdims=True,
        )

    for half in range(2):
        for d in (1, 3, 2):
            g = first((x + NX - d) % NX) + 4 * half
            wait_bytes(o_all.at[c, g], recv_g.at[half, d - 1])
            across(g, 4 * half + d).start()
        for d in range(NX):
            g = first((x + NX - d) % NX) + 4 * half
            wait_bytes(o_all.at[1 - c, g], recv_c.at[4 * half + d])

        projected = None
        for parity in range(NC):
            for zh in range(0, NZ, 2):
                left = jnp.concatenate(
                    [
                        o_all[parity, 4 * half : 4 * half + 4, zh + k].reshape(4 * TOK, DH)
                        for k in range(2)
                    ],
                    axis=1,
                )
                right = jnp.concatenate(
                    [w_all[zh + k, 2 * parity + n] for k in range(2) for n in range(2)], axis=0
                )
                term = jnp.dot(left, right, preferred_element_type=jnp.float32)
                projected = term if projected is None else projected + term

        for g in range(4 * half, 4 * half + 4):
            rows = slice((g % 4) * TOK, (g % 4 + 1) * TOK)
            stream = hid_all[g].astype(jnp.float32) + consts[0, g : g + 1, :] * projected[rows]
            center = jnp.mean(stream, axis=1, keepdims=True)
            apart = stream - center
            spread = jnp.sum(apart * apart, axis=1, keepdims=True)
            scaled = (apart * consts[2, g : g + 1, :]).astype(jnp.bfloat16)
            mixed = lax.dot_general(
                scaled,
                final_buf[...],
                (((1,), (1,)), ((), ())),
                preferred_element_type=jnp.float32,
            )
            message[g, 0 : TOK // 2] = jnp.concatenate(
                [mixed[: TOK // 2], mixed[TOK // 2 :]], axis=1
            )
            both_sums = jnp.concatenate([sums[0, g : g + 1], sums[1, g : g + 1]], axis=1)
            message[g, TOK // 2 :] = jnp.where(
                last_row == 0,
                as_row(center),
                jnp.where(last_row == 1, as_row(spread), both_sums),
            )
            for later in range(2 if g < NQ - 1 else 1):

                @pl.when(queue != g + later)
                def _():
                    remote(
                        message.at[g],
                        received.at[later, queue],
                        send_m.at[later, g],
                        recv_m.at[later, queue],
                        {"queue": g + later, "seq": seq},
                    ).start()

                @pl.when(queue == g + later)
                def _():
                    pltpu.make_async_copy(
                        message.at[g], received.at[later, queue], recv_m.at[later, queue]
                    ).start()

    def velocity_of(later):
        for source in range(NQ):
            wait_bytes(received.at[later, source], recv_m.at[later, source])
        tails = [received[later, source, TOK // 2 :] for source in range(NQ)]
        center = functools.reduce(jnp.add, [tail[0:1] for tail in tails]) / NQ
        spread = functools.reduce(jnp.add, [tail[1:2] for tail in tails])
        mixed = functools.reduce(
            jnp.add, [received[later, source, : TOK // 2] for source in range(NQ)]
        )
        mixed = jnp.concatenate([mixed[:, :LAT], mixed[:, LAT:]], axis=0)
        offset = functools.reduce(jnp.add, [tail[2:3, LAT:] for tail in tails])
        for tail in tails:
            away = tail[0:1] - center
            spread = spread + COLS * (away * away)
            mixed = mixed + as_column(away) * tail[2:3, :LAT]
        return mixed * as_column(1.0 / jnp.sqrt(spread / D + 1e-06)) + offset

    wait_bytes(hid_all.at[pl.ds(0, NQ - 1)], send_h.at[0])
    wait_bytes(act_all.at[pl.ds(0, NQ - 1)], send_h.at[1])
    for array in range(3):
        wait_bytes(q_buf.at[pl.ds(0, 3), pl.ds(0, 5), 0], send_a.at[array])

    @pl.when(xt != x)
    def _():
        wait_bytes(q_buf.at[0, 0, 0], send_a.at[3])

    @pl.when(queue < NQ - 1)
    def _():
        wait_bytes(lat_behind, send_h.at[2])

    for d in range(3):
        wait_bytes(w_all.at[0, 0], send_wy.at[d])
    for side in range(2):
        for array in range(2):
            for n in range(3):
                wait_bytes(k_buf.at[0], send_x.at[array, side, n])
        wait_bytes(q_buf.at[0], send_y.at[side, 0])
        wait_bytes(q_buf.at[0, pl.ds(0, 4)], send_y.at[side, 1])
        for step in range(4):
            wait_bytes(w_all.at[0, pl.ds(0, NY if step < 3 else 2)], send_wz.at[side, step])
    for d in (1, 2, 3):
        for half in range(2):
            wait_bytes(o_part.at[0, 0], send_o.at[half, d - 1])
            wait_bytes(o_all.at[0, 0], send_g.at[half, d - 1])
    wait_bytes(merged.at[pl.ds(0, 7)], send_z.at[0])
    for slot in range(8):
        wait_bytes(o_all.at[0, 0], send_c.at[slot])
    for g in range(NQ):
        for later in range(2 if g < NQ - 1 else 1):

            @pl.when(queue != g + later)
            def _():
                wait_bytes(message.at[0], send_m.at[later, g])

    out_ref[:, 0:LAT] = velocity_of(0)

    @pl.when(queue == 0)
    def _():
        out_ref[:, LAT:] = fresh_buf[...]

    @pl.when(queue > 0)
    def _():
        velocity = velocity_of(1)
        wait_bytes(lat_behind, recv_h.at[2])
        out_ref[:, LAT:] = lat_behind[...] - STRIDE / 1000.0 * velocity


def fused(*operands):
    bf16, f32 = jnp.bfloat16, jnp.float32
    vmem, dma = pltpu.VMEM, pltpu.SemaphoreType.DMA
    in_specs = [pl.BlockSpec(memory_space=pl.ANY)] * 10
    in_specs[5] = pl.BlockSpec(memory_space=pltpu.SMEM)
    return pl.pallas_call(
        fused_kernel,
        out_shape=jax.ShapeDtypeStruct((TOK, 2 * LAT), f32),
        in_specs=in_specs,
        out_specs=pl.BlockSpec(memory_space=pltpu.VMEM),
        scratch_shapes=[
            vmem((NQ, NZ, TOK, DH), bf16),
            vmem((NQ, NZ, TOK, DH), bf16),
            vmem((NY, NQ, 2, TOK, DH), bf16),
            vmem((NQ, NY * ROWS, 256), f32),
            vmem((NQ, NY * ROWS, 128), f32),
            vmem((NY, 2, PART, DH), bf16),
            vmem((NY, 2, PART, DH), bf16),
            vmem((NQ, 2, TOK, DH), bf16),
            vmem((NC, NQ, NZ, TOK, DH), bf16),
            vmem((NQ, TOK, COLS), bf16),
            vmem((NQ, 8, TEMB), f32),
            vmem((NZ, NY, 64, COLS), bf16),
            vmem((3, TEMB, COLS), bf16),
            vmem((LAT, COLS), bf16),
            vmem((TOK, LAT), f32),
            vmem((TOK, LAT), f32),
            vmem((3, NQ, COLS), f32),
            vmem((2, NQ, LAT), f32),
            vmem((NQ, MSG, 128), f32),
            vmem((2, NQ, MSG, 128), f32),
            dma((5,)),
            dma((4,)),
            dma((3,)),
            dma((3,)),
            dma((2, 4)),
            dma((2, 2, 3)),
            dma((2, 2)),
            dma((2, 3)),
            dma((1,)),
            dma((2, 3)),
            dma((8,)),
            dma((2, NQ)),
            dma((2,)),
            dma((2,)),
            dma((1,)),
            dma((3,)),
            dma((1,)),
            dma((2, 4)),
            dma((2, 2, 3)),
            dma((2, 2)),
            dma((2, 3)),
            dma((2,)),
            dma((2, 3)),
            dma((8,)),
            dma((2, NQ)),
        ],
        compiler_params=pltpu.CompilerParams(
            collective_id=0, has_side_effects=True, vmem_limit_bytes=60 * 1024 * 1024
        ),
        name="fused",
    )(*operands)


def body(
    hidden,
    queries,
    keys,
    values,
    timesteps,
    latents,
    fresh_noise,
    out_weight,
    mod_weight,
    final_weight,
):
    result = fused(
        queries[0],
        keys[0],
        values[0],
        hidden[0],
        out_weight,
        timesteps,
        mod_weight,
        final_weight.T,
        latents[0],
        fresh_noise,
    )
    return result[None, :, :LAT], result[None, :, LAT:]


def solution(mesh):
    placed = (
        P("queue", "seq", None),
        P("queue", "seq", None),
        P("queue", "seq", None),
        P("queue", "seq", None),
        P("queue"),
        P("queue", "seq", None),
        P("seq", None),
        P("seq", None),
        P(),
        P(),
    )
    return jax.shard_map(
        body,
        mesh=mesh,
        in_specs=placed,
        out_specs=(P("queue", "seq", None), P("queue", "seq", None)),
        check_vma=False,
    )
```

```python
import functools
import math

import jax
import jax.numpy as jnp
from jax import lax
from jax.experimental import pallas as pl
from jax.experimental.pallas import tpu as pltpu
from jax.sharding import PartitionSpec as P

D = 3072
H = 16
DH = 128
TEMB = 256
STRIDE = 125
NX, NC, NY, NZ = 4, 2, 4, 8
NQ = NX * NC
TOK = 48
COLS = D // NQ
LAT = 64
ROWS = 2 * TOK
PART = 4 * ROWS + 16
MSG = TOK // 2 + 8
SCALE = DH**-0.5 * math.log2(math.e)
MESH = pl.DeviceIdType.MESH


def place(x, c, y, z):
    return {"queue": x * NC + c, "seq": z * NY + y}


def remote(src, dst, send_sem, recv_sem, device):
    return pltpu.make_async_remote_copy(
        src_ref=src,
        dst_ref=dst,
        send_sem=send_sem,
        recv_sem=recv_sem,
        device_id=device,
        device_id_type=MESH,
    )


def wait_bytes(ref, sem):
    pltpu.make_async_copy(ref, ref, sem).wait()


def attend(tasks, q_buf, acc, peak):
    scores = [
        lax.dot_general(
            q_buf[:, i].reshape(NY * ROWS, DH),
            keys,
            (((1,), (1,)), ((), ())),
            preferred_element_type=jnp.float32,
        )
        for i, keys, _ in tasks
    ]
    for (i, _, values), block in zip(tasks, scores):
        extended = jnp.concatenate([values, jnp.ones_like(values)], axis=1)
        weights, factors = [], []
        for part in range(3):
            rows = slice(part * 128, part * 128 + 128)
            piece = block[rows] * SCALE
            old = peak[i, rows, :]
            new = jnp.maximum(old, jnp.max(piece, axis=1, keepdims=True))
            peak[i, rows, :] = new
            factors.append(jnp.exp2(old - new))
            wide = jnp.concatenate([new] * (piece.shape[1] // 128), axis=1)
            weights.append(jnp.exp2(piece - wide).astype(jnp.bfloat16))
        mixed = jnp.dot(
            jnp.concatenate(weights, axis=0), extended, preferred_element_type=jnp.float32
        )
        for part, factor in enumerate(factors):
            rows = slice(part * 128, part * 128 + 128)
            acc[i, rows, :] = (
                acc[i, rows, :] * jnp.concatenate([factor, factor], axis=1) + mixed[rows]
            )


def fused_kernel(
    q_ref,
    k_ref,
    v_ref,
    hid_ref,
    w_ref,
    step_ref,
    mod_ref,
    final_ref,
    lat_ref,
    fresh_ref,
    out_ref,
    k_buf,
    v_buf,
    q_buf,
    acc,
    peak,
    o_part,
    o_recv,
    merged,
    o_all,
    hid_all,
    act_all,
    w_all,
    mod_buf,
    final_buf,
    lat_behind,
    fresh_buf,
    consts,
    sums,
    message,
    received,
    load_sem,
    send_a,
    send_h,
    send_wy,
    send_wz,
    send_x,
    send_y,
    send_o,
    send_z,
    send_g,
    send_c,
    send_m,
    recv_k,
    recv_v,
    recv_q,
    recv_h,
    recv_wy,
    recv_wz,
    recv_x,
    recv_y,
    recv_o,
    recv_z,
    recv_g,
    recv_c,
    recv_m,
):
    queue = lax.axis_index("queue")
    seq = lax.axis_index("seq")
    x, c = queue // NC, queue % NC
    z, y = seq // NY, seq % NY
    xl, xr, x2 = (x + NX - 1) % NX, (x + 1) % NX, (x + 2) % NX
    yl, yr, y2 = (y + NY - 1) % NY, (y + 1) % NY, (y + 2) % NY
    zl, zr = (z + NZ - 1) % NZ, (z + 1) % NZ
    zk = z // 4
    xt = (z + queue) % NX
    own_head = 2 * z + c
    barrier = pltpu.get_barrier_semaphore()

    def greet(j, carry):
        device = place((x + j // 16) % NX, (c + j % 2) % NC, y, (z + (j // 2) % 8) % NZ)
        pl.semaphore_signal(barrier, inc=1, device_id=device, device_id_type=MESH)
        return carry

    lax.fori_loop(1, 64, greet, 0)
    for d in (1, 2, 3):
        pl.semaphore_signal(
            barrier, inc=1, device_id=place(x, c, (y + d) % NY, z), device_id_type=MESH
        )

    def own_columns(part):
        return pl.ds(pl.multiple_of(part * D + queue * COLS, 128), COLS)

    loads = [
        pltpu.make_async_copy(mod_ref.at[:, own_columns(n)], mod_buf.at[n], load_sem.at[n])
        for n in range(3)
    ]
    loads.append(pltpu.make_async_copy(final_ref.at[:, own_columns(0)], final_buf, load_sem.at[3]))
    loads.append(pltpu.make_async_copy(fresh_ref, fresh_buf, load_sem.at[4]))
    for load in loads:
        load.start()

    pl.semaphore_wait(barrier, 66)

    def columns(ref, head):
        return ref.at[:, pl.ds(pl.multiple_of(head * DH, DH), DH)]

    def by_head(array, ref, target, sem, xs):
        def send(j, carry):
            zt, ct = (z + j // 2) % NZ, (c + j % 2) % NC
            remote(
                columns(ref, 2 * zt + ct), target, send_a.at[array], sem, place(xs, ct, y, zt)
            ).start()
            return carry

        lax.fori_loop(1, 16, send, 0)

    by_head(1, q_ref, q_buf.at[y, queue, zk], recv_q.at[0], xt)

    @pl.when(xt != x)
    def _():
        remote(
            columns(q_ref, own_head),
            q_buf.at[y, queue, zk],
            send_a.at[3],
            recv_q.at[0],
            place(xt, c, y, z),
        ).start()

    @pl.when(xt == x)
    def _():
        pltpu.make_async_copy(
            columns(q_ref, own_head), q_buf.at[y, queue, zk], recv_q.at[0]
        ).start()

    by_head(0, k_ref, k_buf.at[queue, z], recv_k.at[c], x)
    pltpu.make_async_copy(columns(k_ref, own_head), k_buf.at[queue, z], recv_k.at[c]).start()
    for d in (1, 2, 3):
        remote(
            w_ref.at[:, own_columns(0)],
            w_all.at[z, y],
            send_wy.at[d - 1],
            recv_wy.at[0],
            place(x, c, (y + d) % NY, z),
        ).start()
    pltpu.make_async_copy(w_ref.at[:, own_columns(0)], w_all.at[z, y], recv_wy.at[0]).start()

    halfway = TEMB // 2
    index = lax.broadcasted_iota(jnp.int32, (8, halfway), 1).astype(jnp.float32)
    angles = step_ref[0].astype(jnp.float32) * jnp.exp(-math.log(10000.0) * index / halfway)
    embed = jnp.concatenate([jnp.cos(angles), jnp.sin(angles)], axis=1)
    act_all[queue] = embed / (1.0 + jnp.exp(-embed))

    def send_act(d, carry):
        to = (queue + d) % NQ
        device = {"queue": to, "seq": seq}
        remote(
            act_all.at[queue], act_all.at[queue], send_h.at[1], recv_h.at[1], device
        ).start()
        return carry

    lax.fori_loop(1, NQ, send_act, 0)

    @pl.when(queue < NQ - 1)
    def _():
        remote(
            lat_ref,
            lat_behind,
            send_h.at[2],
            recv_h.at[2],
            {"queue": (queue + 1) % NQ, "seq": seq},
        ).start()

    acc[...] = jnp.zeros_like(acc)
    peak[...] = jnp.full_like(peak, -1e30)

    def along_x(array, ref):
        for n in range(2):
            for side, to in ((0, xr), (1, xl)):
                blk = n if side == 0 else 1 - n
                block = ref.at[2 * x + blk]
                remote(
                    block,
                    block,
                    send_x.at[array, side, blk],
                    recv_x.at[array, side, blk],
                    place(to, c, y, z),
                ).start()

    def relay_x(array, ref):
        for side, source, to in ((0, xl, xr), (1, xr, xl)):
            block = ref.at[2 * source + side]
            wait_bytes(block, recv_x.at[array, side, side])
            remote(
                block,
                block,
                send_x.at[array, side, 2],
                recv_x.at[array, side, 2],
                place(to, c, y, z),
            ).start()

    wait_bytes(q_buf.at[y], recv_q.at[0])
    for side, to in ((0, yr), (1, yl)):
        remote(
            q_buf.at[y], q_buf.at[y], send_y.at[side, 0], recv_y.at[side, 0], place(x, c, to, z)
        ).start()

    by_head(2, v_ref, v_buf.at[queue, z], recv_v.at[c], x)
    pltpu.make_async_copy(columns(v_ref, own_head), v_buf.at[queue, z], recv_v.at[c]).start()

    for blk in range(2):
        wait_bytes(k_buf.at[2 * x + blk], recv_k.at[blk])
    along_x(0, k_buf)

    for load in loads:
        load.wait()
    wait_bytes(act_all.at[pl.ds(0, NQ - 1)], recv_h.at[1])
    act = act_all[:, 0, :].astype(jnp.bfloat16)
    for n in range(3):
        consts[n] = jnp.dot(act, mod_buf[n], preferred_element_type=jnp.float32)
    consts[2] = 1.0 + consts[2]
    final32 = final_buf[...].astype(jnp.float32)
    for n in range(2):
        sums[n] = lax.dot_general(
            consts[2 - n],
            final32,
            (((1,), (1,)), ((), ())),
            preferred_element_type=jnp.float32,
            precision=lax.Precision.HIGHEST,
        )

    for side, source, to in ((0, yl, yr), (1, yr, yl)):
        wait_bytes(q_buf.at[source], recv_y.at[side, 0])
        slab = q_buf.at[source, pl.ds(4 * side, 4)]
        remote(
            slab, slab, send_y.at[side, 1], recv_y.at[side, 1], place(x, c, to, z)
        ).start()

    for blk in range(2):
        wait_bytes(v_buf.at[2 * x + blk], recv_v.at[blk])
    along_x(1, v_buf)
    relay_x(0, k_buf)

    def send_hidden(d, carry):
        to = (queue + d) % NQ
        remote(
            hid_ref.at[:, pl.ds(pl.multiple_of(to * COLS, 128), COLS)],
            hid_all.at[queue],
            send_h.at[0],
            recv_h.at[0],
            {"queue": to, "seq": seq},
        ).start()
        return carry

    def ring_z(step):
        for side, to in ((0, zr), (1, zl)):
            back = NZ - step if side == 0 else step
            rows = pl.ds(0, NY) if step < 3 else pl.ds(2 * side, 2)
            chunk = w_all.at[(z + back) % NZ]
            if step:
                wait_bytes(chunk, recv_wz.at[side, step - 1])
            chunk = w_all.at[(z + back) % NZ, rows]
            remote(
                chunk,
                chunk,
                send_wz.at[side, step],
                recv_wz.at[side, step],
                place(x, c, y, to),
            ).start()

    wait_bytes(w_all.at[z], recv_wy.at[0])
    ring_z(0)
    for side in range(2):
        wait_bytes(q_buf.at[y2, pl.ds(4 * side, 4)], recv_y.at[side, 1])

    lane = lax.broadcasted_iota(jnp.int32, (ROWS, 128), 1)
    row = lax.broadcasted_iota(jnp.int32, (ROWS, 128), 0)
    diagonal = lane == row
    stat_row = lax.broadcasted_iota(jnp.int32, (16, 128), 0)

    def finish(half):
        vectors = [[] for _ in range(NY)]
        for k in range(4):
            g = 4 * half + k
            total = acc[g, :, 128:]
            out = (acc[g, :, :128] / total).astype(jnp.bfloat16)
            level = peak[g] + jnp.log2(total)
            for part in range(NY):
                rows = slice(part * ROWS, (part + 1) * ROWS)
                vector = jnp.sum(jnp.where(diagonal, level[rows], 0.0), axis=0, keepdims=True)
                high = vector.astype(jnp.bfloat16).astype(jnp.float32)
                middle = (vector - high).astype(jnp.bfloat16).astype(jnp.float32)
                vectors[part] += [high, middle, vector - high - middle]
                o_part[part, half, k * ROWS : (k + 1) * ROWS] = out[rows]
        for part in range(NY):
            stats = jnp.zeros((16, 128), jnp.float32)
            for n, vector in enumerate(vectors[part]):
                stats = jnp.where(stat_row == n, vector, stats)
            o_part[part, half, 4 * ROWS :] = stats.astype(jnp.bfloat16)

    def partial_copy(half, d):
        to = (y + d) % NY
        return remote(
            o_part.at[to, half],
            o_recv.at[y, half],
            send_o.at[half, d - 1],
            recv_o.at[half, d - 1],
            place(x, c, to, z),
        )

    key_rows = NZ * TOK

    def stage(st, carry):
        p = (x + st + st // 2 - 2 * (st // 3)) % NX

        @pl.when(st == 1)
        def _():
            relay_x(1, v_buf)
            for ref, array in ((k_buf, 0), (v_buf, 1)):
                wait_bytes(ref.at[2 * xr], recv_x.at[array, 1, 0])

        @pl.when(st == 2)
        def _():
            ring_z(1)
            lax.fori_loop(1, NQ, send_hidden, 0)
            pltpu.make_async_copy(
                hid_ref.at[:, own_columns(0)], hid_all.at[queue], recv_h.at[0]
            ).start()
            for ref, array in ((k_buf, 0), (v_buf, 1)):
                wait_bytes(ref.at[2 * xl + 1], recv_x.at[array, 0, 1])

        @pl.when(st == 3)
        def _():
            for ref, array in ((k_buf, 0), (v_buf, 1)):
                for side in range(2):
                    wait_bytes(ref.at[2 * x2 + side], recv_x.at[array, side, 2])

        high, odd = p // 2, p % 2

        def both(j, carry):
            keys = k_buf[pl.ds(2 * p, 2)].reshape(2 * key_rows, DH)
            values = v_buf[pl.ds(2 * p, 2)].reshape(2 * key_rows, DH)
            attend([(2 * j, keys, values), (2 * j + 1, keys, values)], q_buf, acc, peak)
            return carry

        def halves(half, carry):
            same = 1 - (high - half) * (high - half)
            count = 2 * high * (1 - half) + odd * same
            lax.fori_loop(2 * half, 2 * half + count, both, 0)

            @pl.when(high == half)
            def _():
                keys = k_buf[pl.ds(2 * p, 2)].reshape(2 * key_rows, DH)
                values = v_buf[pl.ds(2 * p, 2)].reshape(2 * key_rows, DH)
                attend(
                    [
                        (2 * p, keys, values),
                        (2 * p + 1, keys[key_rows:], values[key_rows:]),
                    ],
                    q_buf,
                    acc,
                    peak,
                )

            @pl.when(st == 3)
            def _():
                finish(half)
                for d in (2, 1, 3):
                    partial_copy(half, d).start()

                @pl.when(half == 0)
                def _():
                    ring_z(2)

            return carry

        return lax.fori_loop(0, 2, halves, carry)

    lax.fori_loop(0, 4, stage, 0)
    ring_z(3)

    def column(vector):
        return jnp.sum(
            jnp.where(diagonal, jnp.broadcast_to(vector, (ROWS, 128)), 0.0),
            axis=1,
            keepdims=True,
        )

    def merge(half):
        refs = [o_part.at[y, half]] + [o_recv.at[(y + d) % NY, half] for d in (1, 2, 3)]
        stats = [ref[4 * ROWS :].astype(jnp.float32) for ref in refs]
        for k in range(4):
            g = 4 * half + k
            levels = [
                column(stat[3 * k : 3 * k + 1] + stat[3 * k + 1 : 3 * k + 2] + stat[3 * k + 2 : 3 * k + 3])
                for stat in stats
            ]
            top = functools.reduce(jnp.maximum, levels)
            shares = [jnp.exp2(level - top) for level in levels]
            total = functools.reduce(jnp.add, shares)
            mixed = functools.reduce(
                jnp.add,
                [
                    share * ref[k * ROWS : (k + 1) * ROWS].astype(jnp.float32)
                    for share, ref in zip(shares, refs)
                ],
            )
            merged[g] = (mixed / total).astype(jnp.bfloat16).reshape(2, TOK, DH)
            for n in range(2):
                zt = (x + 8 - g) % 4 + 4 * n

                @pl.when(zt != z)
                def _():
                    remote(
                        merged.at[g, n],
                        o_all.at[c, g, z],
                        send_z.at[0],
                        recv_z.at[half],
                        place(x, c, y, zt),
                    ).start()

                @pl.when(zt == z)
                def _():
                    pltpu.make_async_copy(
                        merged.at[g, n], o_all.at[c, g, z], recv_z.at[half]
                    ).start()

    def first(xs):
        return (xs + 8 - z) % 4

    def across(g, slot):
        return remote(
            o_all.at[c, g],
            o_all.at[c, g],
            send_c.at[slot],
            recv_c.at[slot],
            place(x, 1 - c, y, z),
        )

    for half in range(2):
        for d in (1, 3, 2):
            wait_bytes(o_recv.at[(y + NY - d) % NY, half], recv_o.at[half, d - 1])
        merge(half)
    for half in range(2):
        g = first(x) + 4 * half
        wait_bytes(o_all.at[c, g], recv_z.at[half])
        for d in (2, 1, 3):
            remote(
                o_all.at[c, g],
                o_all.at[c, g],
                send_g.at[half, d - 1],
                recv_g.at[half, d - 1],
                place((x + d) % NX, c, y, z),
            ).start()
        across(g, 4 * half).start()

    wait_bytes(hid_all, recv_h.at[0])
    for side in range(2):
        wait_bytes(w_all.at[(z + 4) % NZ, pl.ds(2 * side, 2)], recv_wz.at[side, 3])

    token_lane = lax.broadcasted_iota(jnp.int32, (TOK, 128), 1)
    token_row = lax.broadcasted_iota(jnp.int32, (TOK, 128), 0)
    token_diagonal = token_lane == token_row
    last_row = lax.broadcasted_iota(jnp.int32, (8, 128), 0)

    def as_row(vector):
        return jnp.sum(
            jnp.where(token_diagonal, jnp.broadcast_to(vector, (TOK, 128)), 0.0),
            axis=0,
            keepdims=True,
        )

    def as_column(vector):
        return jnp.sum(
            jnp.where(token_diagonal, jnp.broadcast_to(vector, (TOK, 128)), 0.0),
            axis=1,
            keepdims=True,
        )

    for half in range(2):
        for d in (1, 3, 2):
            g = first((x + NX - d) % NX) + 4 * half
            wait_bytes(o_all.at[c, g], recv_g.at[half, d - 1])
            across(g, 4 * half + d).start()
        for d in range(NX):
            g = first((x + NX - d) % NX) + 4 * half
            wait_bytes(o_all.at[1 - c, g], recv_c.at[4 * half + d])

        projected = None
        for parity in range(NC):
            for zh in range(0, NZ, 2):
                left = jnp.concatenate(
                    [
                        o_all[parity, 4 * half : 4 * half + 4, zh + k].reshape(4 * TOK, DH)
                        for k in range(2)
                    ],
                    axis=1,
                )
                right = jnp.concatenate(
                    [w_all[zh + k, 2 * parity + n] for k in range(2) for n in range(2)], axis=0
                )
                term = jnp.dot(left, right, preferred_element_type=jnp.float32)
                projected = term if projected is None else projected + term

        for g in range(4 * half, 4 * half + 4):
            rows = slice((g % 4) * TOK, (g % 4 + 1) * TOK)
            stream = hid_all[g].astype(jnp.float32) + consts[0, g : g + 1, :] * projected[rows]
            center = jnp.mean(stream, axis=1, keepdims=True)
            apart = stream - center
            spread = jnp.sum(apart * apart, axis=1, keepdims=True)
            scaled = (apart * consts[2, g : g + 1, :]).astype(jnp.bfloat16)
            mixed = lax.dot_general(
                scaled,
                final_buf[...],
                (((1,), (1,)), ((), ())),
                preferred_element_type=jnp.float32,
            )
            message[g, 0 : TOK // 2] = jnp.concatenate(
                [mixed[: TOK // 2], mixed[TOK // 2 :]], axis=1
            )
            both_sums = jnp.concatenate([sums[0, g : g + 1], sums[1, g : g + 1]], axis=1)
            message[g, TOK // 2 :] = jnp.where(
                last_row == 0,
                as_row(center),
                jnp.where(last_row == 1, as_row(spread), both_sums),
            )
            for later in range(2 if g < NQ - 1 else 1):

                @pl.when(queue != g + later)
                def _():
                    remote(
                        message.at[g],
                        received.at[later, queue],
                        send_m.at[later, g],
                        recv_m.at[later, queue],
                        {"queue": g + later, "seq": seq},
                    ).start()

                @pl.when(queue == g + later)
                def _():
                    pltpu.make_async_copy(
                        message.at[g], received.at[later, queue], recv_m.at[later, queue]
                    ).start()

    def velocity_of(later):
        for source in range(NQ):
            wait_bytes(received.at[later, source], recv_m.at[later, source])
        tails = [received[later, source, TOK // 2 :] for source in range(NQ)]
        center = functools.reduce(jnp.add, [tail[0:1] for tail in tails]) / NQ
        spread = functools.reduce(jnp.add, [tail[1:2] for tail in tails])
        mixed = functools.reduce(
            jnp.add, [received[later, source, : TOK // 2] for source in range(NQ)]
        )
        mixed = jnp.concatenate([mixed[:, :LAT], mixed[:, LAT:]], axis=0)
        offset = functools.reduce(jnp.add, [tail[2:3, LAT:] for tail in tails])
        for tail in tails:
            away = tail[0:1] - center
            spread = spread + COLS * (away * away)
            mixed = mixed + as_column(away) * tail[2:3, :LAT]
        return mixed * as_column(1.0 / jnp.sqrt(spread / D + 1e-06)) + offset

    wait_bytes(hid_all.at[pl.ds(0, NQ - 1)], send_h.at[0])
    wait_bytes(act_all.at[pl.ds(0, NQ - 1)], send_h.at[1])
    for array in range(3):
        wait_bytes(q_buf.at[pl.ds(0, 3), pl.ds(0, 5), 0], send_a.at[array])

    @pl.when(xt != x)
    def _():
        wait_bytes(q_buf.at[0, 0, 0], send_a.at[3])

    @pl.when(queue < NQ - 1)
    def _():
        wait_bytes(lat_behind, send_h.at[2])

    for d in range(3):
        wait_bytes(w_all.at[0, 0], send_wy.at[d])
    for side in range(2):
        for array in range(2):
            for n in range(3):
                wait_bytes(k_buf.at[0], send_x.at[array, side, n])
        wait_bytes(q_buf.at[0], send_y.at[side, 0])
        wait_bytes(q_buf.at[0, pl.ds(0, 4)], send_y.at[side, 1])
        for step in range(4):
            wait_bytes(w_all.at[0, pl.ds(0, NY if step < 3 else 2)], send_wz.at[side, step])
    for d in (1, 2, 3):
        for half in range(2):
            wait_bytes(o_part.at[0, 0], send_o.at[half, d - 1])
            wait_bytes(o_all.at[0, 0], send_g.at[half, d - 1])
    wait_bytes(merged.at[pl.ds(0, 7)], send_z.at[0])
    for slot in range(8):
        wait_bytes(o_all.at[0, 0], send_c.at[slot])
    for g in range(NQ):
        for later in range(2 if g < NQ - 1 else 1):

            @pl.when(queue != g + later)
            def _():
                wait_bytes(message.at[0], send_m.at[later, g])

    out_ref[:, 0:LAT] = velocity_of(0)

    @pl.when(queue == 0)
    def _():
        out_ref[:, LAT:] = fresh_buf[...]

    @pl.when(queue > 0)
    def _():
        velocity = velocity_of(1)
        wait_bytes(lat_behind, recv_h.at[2])
        out_ref[:, LAT:] = lat_behind[...] - STRIDE / 1000.0 * velocity


def fused(*operands):
    bf16, f32 = jnp.bfloat16, jnp.float32
    vmem, dma = pltpu.VMEM, pltpu.SemaphoreType.DMA
    in_specs = [pl.BlockSpec(memory_space=pl.ANY)] * 10
    in_specs[5] = pl.BlockSpec(memory_space=pltpu.SMEM)
    return pl.pallas_call(
        fused_kernel,
        out_shape=jax.ShapeDtypeStruct((TOK, 2 * LAT), f32),
        in_specs=in_specs,
        out_specs=pl.BlockSpec(memory_space=pltpu.VMEM),
        scratch_shapes=[
            vmem((NQ, NZ, TOK, DH), bf16),
            vmem((NQ, NZ, TOK, DH), bf16),
            vmem((NY, NQ, 2, TOK, DH), bf16),
            vmem((NQ, NY * ROWS, 256), f32),
            vmem((NQ, NY * ROWS, 128), f32),
            vmem((NY, 2, PART, DH), bf16),
            vmem((NY, 2, PART, DH), bf16),
            vmem((NQ, 2, TOK, DH), bf16),
            vmem((NC, NQ, NZ, TOK, DH), bf16),
            vmem((NQ, TOK, COLS), bf16),
            vmem((NQ, 8, TEMB), f32),
            vmem((NZ, NY, 64, COLS), bf16),
            vmem((3, TEMB, COLS), bf16),
            vmem((LAT, COLS), bf16),
            vmem((TOK, LAT), f32),
            vmem((TOK, LAT), f32),
            vmem((3, NQ, COLS), f32),
            vmem((2, NQ, LAT), f32),
            vmem((NQ, MSG, 128), f32),
            vmem((2, NQ, MSG, 128), f32),
            dma((5,)),
            dma((4,)),
            dma((3,)),
            dma((3,)),
            dma((2, 4)),
            dma((2, 2, 3)),
            dma((2, 2)),
            dma((2, 3)),
            dma((1,)),
            dma((2, 3)),
            dma((8,)),
            dma((2, NQ)),
            dma((2,)),
            dma((2,)),
            dma((1,)),
            dma((3,)),
            dma((1,)),
            dma((2, 4)),
            dma((2, 2, 3)),
            dma((2, 2)),
            dma((2, 3)),
            dma((2,)),
            dma((2, 3)),
            dma((8,)),
            dma((2, NQ)),
        ],
        compiler_params=pltpu.CompilerParams(
            collective_id=0, has_side_effects=True, vmem_limit_bytes=60 * 1024 * 1024
        ),
        name="fused",
    )(*operands)


def body(
    hidden,
    queries,
    keys,
    values,
    timesteps,
    latents,
    fresh_noise,
    out_weight,
    mod_weight,
    final_weight,
):
    result = fused(
        queries[0],
        keys[0],
        values[0],
        hidden[0],
        out_weight,
        timesteps,
        mod_weight,
        final_weight.T,
        latents[0],
        fresh_noise,
    )
    return result[None, :, :LAT], result[None, :, LAT:]


def solution(mesh):
    placed = (
        P("queue", "seq", None),
        P("queue", "seq", None),
        P("queue", "seq", None),
        P("queue", "seq", None),
        P("queue"),
        P("queue", "seq", None),
        P("seq", None),
        P("seq", None),
        P(),
        P(),
    )
    return jax.shard_map(
        body,
        mesh=mesh,
        in_specs=placed,
        out_specs=(P("queue", "seq", None), P("queue", "seq", None)),
        check_vma=False,
    )
```

```python
import functools
import math

import jax
import jax.numpy as jnp
from jax import lax
from jax.experimental import pallas as pl
from jax.experimental.pallas import tpu as pltpu
from jax.sharding import PartitionSpec as P

D = 3072
H = 16
DH = 128
TEMB = 256
STRIDE = 125
NX, NC, NY, NZ = 4, 2, 4, 8
NQ = NX * NC
TOK = 48
COLS = D // NQ
LAT = 64
ROWS = 2 * TOK
PART = 4 * ROWS + 16
MSG = TOK // 2 + 8
SCALE = DH**-0.5 * math.log2(math.e)
MESH = pl.DeviceIdType.MESH


def place(x, c, y, z):
    return {"queue": x * NC + c, "seq": z * NY + y}


def remote(src, dst, send_sem, recv_sem, device):
    return pltpu.make_async_remote_copy(
        src_ref=src,
        dst_ref=dst,
        send_sem=send_sem,
        recv_sem=recv_sem,
        device_id=device,
        device_id_type=MESH,
    )


def wait_bytes(ref, sem):
    pltpu.make_async_copy(ref, ref, sem).wait()


def attend(tasks, q_buf, acc, peak):
    scores = [
        lax.dot_general(
            q_buf[:, i].reshape(NY * ROWS, DH),
            keys,
            (((1,), (1,)), ((), ())),
            preferred_element_type=jnp.float32,
        )
        for i, keys, _ in tasks
    ]
    for (i, _, values), block in zip(tasks, scores):
        extended = jnp.concatenate([values, jnp.ones_like(values)], axis=1)
        weights, factors = [], []
        for part in range(3):
            rows = slice(part * 128, part * 128 + 128)
            piece = block[rows] * SCALE
            old = peak[i, rows, :]
            new = jnp.maximum(old, jnp.max(piece, axis=1, keepdims=True))
            peak[i, rows, :] = new
            factors.append(jnp.exp2(old - new))
            wide = jnp.concatenate([new] * (piece.shape[1] // 128), axis=1)
            weights.append(jnp.exp2(piece - wide).astype(jnp.bfloat16))
        mixed = jnp.dot(
            jnp.concatenate(weights, axis=0), extended, preferred_element_type=jnp.float32
        )
        for part, factor in enumerate(factors):
            rows = slice(part * 128, part * 128 + 128)
            acc[i, rows, :] = (
                acc[i, rows, :] * jnp.concatenate([factor, factor], axis=1) + mixed[rows]
            )


def fused_kernel(
    q_ref,
    k_ref,
    v_ref,
    hid_ref,
    w_ref,
    step_ref,
    mod_ref,
    final_ref,
    lat_ref,
    fresh_ref,
    out_ref,
    k_buf,
    v_buf,
    q_buf,
    acc,
    peak,
    o_part,
    o_recv,
    merged,
    o_all,
    hid_all,
    act_all,
    w_all,
    mod_buf,
    final_buf,
    lat_behind,
    fresh_buf,
    consts,
    sums,
    message,
    received,
    load_sem,
    send_a,
    send_h,
    send_wy,
    send_wz,
    send_x,
    send_y,
    send_o,
    send_z,
    send_g,
    send_c,
    send_m,
    recv_k,
    recv_v,
    recv_q,
    recv_h,
    recv_wy,
    recv_wz,
    recv_x,
    recv_y,
    recv_o,
    recv_z,
    recv_g,
    recv_c,
    recv_m,
):
    queue = lax.axis_index("queue")
    seq = lax.axis_index("seq")
    x, c = queue // NC, queue % NC
    z, y = seq // NY, seq % NY
    xl, xr, x2 = (x + NX - 1) % NX, (x + 1) % NX, (x + 2) % NX
    yl, yr, y2 = (y + NY - 1) % NY, (y + 1) % NY, (y + 2) % NY
    zl, zr = (z + NZ - 1) % NZ, (z + 1) % NZ
    zk = z // 4
    xt = (z + queue) % NX
    own_head = 2 * z + c
    barrier = pltpu.get_barrier_semaphore()

    queues = [(queue + d) % NQ for d in range(NQ)]
    seqs = [(seq + d * NY) % (NY * NZ) for d in range(NZ)]
    for d, q2 in enumerate(queues):
        for e, s2 in enumerate(seqs):
            if d or e:
                pl.semaphore_signal(
                    barrier, inc=1, device_id={"queue": q2, "seq": s2}, device_id_type=MESH
                )
    for d in (1, 2, 3):
        pl.semaphore_signal(
            barrier, inc=1, device_id=place(x, c, (y + d) % NY, z), device_id_type=MESH
        )

    def own_columns(part):
        return pl.ds(pl.multiple_of(part * D + queue * COLS, 128), COLS)

    loads = [
        pltpu.make_async_copy(mod_ref.at[:, own_columns(n)], mod_buf.at[n], load_sem.at[n])
        for n in range(3)
    ]
    loads.append(pltpu.make_async_copy(final_ref.at[:, own_columns(0)], final_buf, load_sem.at[3]))
    loads.append(pltpu.make_async_copy(fresh_ref, fresh_buf, load_sem.at[4]))
    for load in loads:
        load.start()

    pl.semaphore_wait(barrier, 66)

    def columns(ref, head):
        return ref.at[:, pl.ds(pl.multiple_of(head * DH, DH), DH)]

    def by_head(array, ref, target, sem, xs):
        for n in range(1, 16):
            zt, ct = zs[n // 2], cs[n % 2]
            remote(
                columns(ref, 2 * zt + ct),
                target,
                send_a.at[array],
                sem,
                {"queue": xs * NC + ct, "seq": seqs[n // 2]},
            ).start()

    zs = [(z + d) % NZ for d in range(NZ)]
    cs = [c, 1 - c]
    by_head(1, q_ref, q_buf.at[y, queue, zk], recv_q.at[0], xt)

    @pl.when(xt != x)
    def _():
        remote(
            columns(q_ref, own_head),
            q_buf.at[y, queue, zk],
            send_a.at[3],
            recv_q.at[0],
            place(xt, c, y, z),
        ).start()

    @pl.when(xt == x)
    def _():
        pltpu.make_async_copy(
            columns(q_ref, own_head), q_buf.at[y, queue, zk], recv_q.at[0]
        ).start()

    by_head(0, k_ref, k_buf.at[queue, z], recv_k.at[c], x)
    pltpu.make_async_copy(columns(k_ref, own_head), k_buf.at[queue, z], recv_k.at[c]).start()
    for d in (1, 2, 3):
        remote(
            w_ref.at[:, own_columns(0)],
            w_all.at[z, y],
            send_wy.at[d - 1],
            recv_wy.at[0],
            place(x, c, (y + d) % NY, z),
        ).start()
    pltpu.make_async_copy(w_ref.at[:, own_columns(0)], w_all.at[z, y], recv_wy.at[0]).start()

    halfway = TEMB // 2
    index = lax.broadcasted_iota(jnp.int32, (8, halfway), 1).astype(jnp.float32)
    angles = step_ref[0].astype(jnp.float32) * jnp.exp(-math.log(10000.0) * index / halfway)
    embed = jnp.concatenate([jnp.cos(angles), jnp.sin(angles)], axis=1)
    act_all[queue] = embed / (1.0 + jnp.exp(-embed))

    for to in queues[1:]:
        remote(
            act_all.at[queue],
            act_all.at[queue],
            send_h.at[1],
            recv_h.at[1],
            {"queue": to, "seq": seq},
        ).start()

    @pl.when(queue < NQ - 1)
    def _():
        remote(
            lat_ref,
            lat_behind,
            send_h.at[2],
            recv_h.at[2],
            {"queue": (queue + 1) % NQ, "seq": seq},
        ).start()

    acc[...] = jnp.zeros_like(acc)
    peak[...] = jnp.full_like(peak, -1e30)

    def along_x(array, ref):
        for n in range(2):
            for side, to in ((0, xr), (1, xl)):
                blk = n if side == 0 else 1 - n
                block = ref.at[2 * x + blk]
                remote(
                    block,
                    block,
                    send_x.at[array, side, blk],
                    recv_x.at[array, side, blk],
                    place(to, c, y, z),
                ).start()

    def relay_x(array, ref):
        for side, source, to in ((0, xl, xr), (1, xr, xl)):
            block = ref.at[2 * source + side]
            wait_bytes(block, recv_x.at[array, side, side])
            remote(
                block,
                block,
                send_x.at[array, side, 2],
                recv_x.at[array, side, 2],
                place(to, c, y, z),
            ).start()

    wait_bytes(q_buf.at[y], recv_q.at[0])
    for side, to in ((0, yr), (1, yl)):
        remote(
            q_buf.at[y], q_buf.at[y], send_y.at[side, 0], recv_y.at[side, 0], place(x, c, to, z)
        ).start()

    by_head(2, v_ref, v_buf.at[queue, z], recv_v.at[c], x)
    pltpu.make_async_copy(columns(v_ref, own_head), v_buf.at[queue, z], recv_v.at[c]).start()

    for blk in range(2):
        wait_bytes(k_buf.at[2 * x + blk], recv_k.at[blk])
    along_x(0, k_buf)

    for load in loads:
        load.wait()
    wait_bytes(act_all.at[pl.ds(0, NQ - 1)], recv_h.at[1])
    act = act_all[:, 0, :].astype(jnp.bfloat16)
    for n in range(3):
        consts[n] = jnp.dot(act, mod_buf[n], preferred_element_type=jnp.float32)
    consts[2] = 1.0 + consts[2]
    final32 = final_buf[...].astype(jnp.float32)
    for n in range(2):
        sums[n] = lax.dot_general(
            consts[2 - n],
            final32,
            (((1,), (1,)), ((), ())),
            preferred_element_type=jnp.float32,
            precision=lax.Precision.HIGHEST,
        )

    for side, source, to in ((0, yl, yr), (1, yr, yl)):
        wait_bytes(q_buf.at[source], recv_y.at[side, 0])
        slab = q_buf.at[source, pl.ds(4 * side, 4)]
        remote(
            slab, slab, send_y.at[side, 1], recv_y.at[side, 1], place(x, c, to, z)
        ).start()

    for blk in range(2):
        wait_bytes(v_buf.at[2 * x + blk], recv_v.at[blk])
    along_x(1, v_buf)
    relay_x(0, k_buf)

    def send_hidden(d, carry):
        to = (queue + d) % NQ
        remote(
            hid_ref.at[:, pl.ds(pl.multiple_of(to * COLS, 128), COLS)],
            hid_all.at[queue],
            send_h.at[0],
            recv_h.at[0],
            {"queue": to, "seq": seq},
        ).start()
        return carry

    def ring_z(step):
        for side, to in ((0, zr), (1, zl)):
            back = NZ - step if side == 0 else step
            rows = pl.ds(0, NY) if step < 3 else pl.ds(2 * side, 2)
            chunk = w_all.at[(z + back) % NZ]
            if step:
                wait_bytes(chunk, recv_wz.at[side, step - 1])
            chunk = w_all.at[(z + back) % NZ, rows]
            remote(
                chunk,
                chunk,
                send_wz.at[side, step],
                recv_wz.at[side, step],
                place(x, c, y, to),
            ).start()

    wait_bytes(w_all.at[z], recv_wy.at[0])
    ring_z(0)
    for side in range(2):
        wait_bytes(q_buf.at[y2, pl.ds(4 * side, 4)], recv_y.at[side, 1])

    lane = lax.broadcasted_iota(jnp.int32, (ROWS, 128), 1)
    row = lax.broadcasted_iota(jnp.int32, (ROWS, 128), 0)
    diagonal = lane == row
    stat_row = lax.broadcasted_iota(jnp.int32, (16, 128), 0)

    def finish(half):
        vectors = [[] for _ in range(NY)]
        for k in range(4):
            g = 4 * half + k
            total = acc[g, :, 128:]
            out = (acc[g, :, :128] / total).astype(jnp.bfloat16)
            level = peak[g] + jnp.log2(total)
            for part in range(NY):
                rows = slice(part * ROWS, (part + 1) * ROWS)
                vector = jnp.sum(jnp.where(diagonal, level[rows], 0.0), axis=0, keepdims=True)
                high = vector.astype(jnp.bfloat16).astype(jnp.float32)
                middle = (vector - high).astype(jnp.bfloat16).astype(jnp.float32)
                vectors[part] += [high, middle, vector - high - middle]
                o_part[part, half, k * ROWS : (k + 1) * ROWS] = out[rows]
        for part in range(NY):
            stats = jnp.zeros((16, 128), jnp.float32)
            for n, vector in enumerate(vectors[part]):
                stats = jnp.where(stat_row == n, vector, stats)
            o_part[part, half, 4 * ROWS :] = stats.astype(jnp.bfloat16)

    def partial_copy(half, d):
        to = (y + d) % NY
        return remote(
            o_part.at[to, half],
            o_recv.at[y, half],
            send_o.at[half, d - 1],
            recv_o.at[half, d - 1],
            place(x, c, to, z),
        )

    key_rows = NZ * TOK

    def stage(st, carry):
        p = (x + st + st // 2 - 2 * (st // 3)) % NX

        @pl.when(st == 1)
        def _():
            relay_x(1, v_buf)
            for ref, array in ((k_buf, 0), (v_buf, 1)):
                wait_bytes(ref.at[2 * xr], recv_x.at[array, 1, 0])

        @pl.when(st == 2)
        def _():
            ring_z(1)
            lax.fori_loop(1, NQ, send_hidden, 0)
            pltpu.make_async_copy(
                hid_ref.at[:, own_columns(0)], hid_all.at[queue], recv_h.at[0]
            ).start()
            for ref, array in ((k_buf, 0), (v_buf, 1)):
                wait_bytes(ref.at[2 * xl + 1], recv_x.at[array, 0, 1])

        @pl.when(st == 3)
        def _():
            for ref, array in ((k_buf, 0), (v_buf, 1)):
                for side in range(2):
                    wait_bytes(ref.at[2 * x2 + side], recv_x.at[array, side, 2])

        high, odd = p // 2, p % 2

        def both(j, carry):
            keys = k_buf[pl.ds(2 * p, 2)].reshape(2 * key_rows, DH)
            values = v_buf[pl.ds(2 * p, 2)].reshape(2 * key_rows, DH)
            attend([(2 * j, keys, values), (2 * j + 1, keys, values)], q_buf, acc, peak)
            return carry

        def halves(half, carry):
            same = 1 - (high - half) * (high - half)
            count = 2 * high * (1 - half) + odd * same
            lax.fori_loop(2 * half, 2 * half + count, both, 0)

            @pl.when(high == half)
            def _():
                keys = k_buf[pl.ds(2 * p, 2)].reshape(2 * key_rows, DH)
                values = v_buf[pl.ds(2 * p, 2)].reshape(2 * key_rows, DH)
                attend(
                    [
                        (2 * p, keys, values),
                        (2 * p + 1, keys[key_rows:], values[key_rows:]),
                    ],
                    q_buf,
                    acc,
                    peak,
                )

            @pl.when(st == 3)
            def _():
                finish(half)
                for d in (2, 1, 3):
                    partial_copy(half, d).start()

                @pl.when(half == 0)
                def _():
                    ring_z(2)

            return carry

        return lax.fori_loop(0, 2, halves, carry)

    lax.fori_loop(0, 4, stage, 0)
    ring_z(3)

    def column(vector):
        return jnp.sum(
            jnp.where(diagonal, jnp.broadcast_to(vector, (ROWS, 128)), 0.0),
            axis=1,
            keepdims=True,
        )

    def merge(half):
        refs = [o_part.at[y, half]] + [o_recv.at[(y + d) % NY, half] for d in (1, 2, 3)]
        stats = [ref[4 * ROWS :].astype(jnp.float32) for ref in refs]
        for k in range(4):
            g = 4 * half + k
            levels = [
                column(stat[3 * k : 3 * k + 1] + stat[3 * k + 1 : 3 * k + 2] + stat[3 * k + 2 : 3 * k + 3])
                for stat in stats
            ]
            top = functools.reduce(jnp.maximum, levels)
            shares = [jnp.exp2(level - top) for level in levels]
            total = functools.reduce(jnp.add, shares)
            mixed = functools.reduce(
                jnp.add,
                [
                    share * ref[k * ROWS : (k + 1) * ROWS].astype(jnp.float32)
                    for share, ref in zip(shares, refs)
                ],
            )
            merged[g] = (mixed / total).astype(jnp.bfloat16).reshape(2, TOK, DH)
        for k in range(4):
            g = 4 * half + k
            for n in range(2):
                zt = (x + 8 - g) % 4 + 4 * n

                @pl.when(zt != z)
                def _():
                    remote(
                        merged.at[g, n],
                        o_all.at[c, g, z],
                        send_z.at[0],
                        recv_z.at[half],
                        place(x, c, y, zt),
                    ).start()

                @pl.when(zt == z)
                def _():
                    pltpu.make_async_copy(
                        merged.at[g, n], o_all.at[c, g, z], recv_z.at[half]
                    ).start()

    def first(xs):
        return (xs + 8 - z) % 4

    def across(g, slot):
        return remote(
            o_all.at[c, g],
            o_all.at[c, g],
            send_c.at[slot],
            recv_c.at[slot],
            place(x, 1 - c, y, z),
        )

    for half in range(2):
        for d in (1, 3, 2):
            wait_bytes(o_recv.at[(y + NY - d) % NY, half], recv_o.at[half, d - 1])
        merge(half)
    for half in range(2):
        g = first(x) + 4 * half
        wait_bytes(o_all.at[c, g], recv_z.at[half])
        for d in (2, 1, 3):
            remote(
                o_all.at[c, g],
                o_all.at[c, g],
                send_g.at[half, d - 1],
                recv_g.at[half, d - 1],
                place((x + d) % NX, c, y, z),
            ).start()
        across(g, 4 * half).start()

    wait_bytes(hid_all, recv_h.at[0])
    for side in range(2):
        wait_bytes(w_all.at[(z + 4) % NZ, pl.ds(2 * side, 2)], recv_wz.at[side, 3])

    token_lane = lax.broadcasted_iota(jnp.int32, (TOK, 128), 1)
    token_row = lax.broadcasted_iota(jnp.int32, (TOK, 128), 0)
    token_diagonal = token_lane == token_row
    last_row = lax.broadcasted_iota(jnp.int32, (8, 128), 0)

    def as_row(vector):
        return jnp.sum(
            jnp.where(token_diagonal, jnp.broadcast_to(vector, (TOK, 128)), 0.0),
            axis=0,
            keepdims=True,
        )

    def as_column(vector):
        return jnp.sum(
            jnp.where(token_diagonal, jnp.broadcast_to(vector, (TOK, 128)), 0.0),
            axis=1,
            keepdims=True,
        )

    for half in range(2):
        for d in (1, 3, 2):
            g = first((x + NX - d) % NX) + 4 * half
            wait_bytes(o_all.at[c, g], recv_g.at[half, d - 1])
            across(g, 4 * half + d).start()
        projected = None
        for parity in (c, 1 - c):
            if projected is not None:
                for d in range(NX):
                    g = first((x + NX - d) % NX) + 4 * half
                    wait_bytes(o_all.at[parity, g], recv_c.at[4 * half + d])
            for zh in range(0, NZ, 2):
                left = jnp.concatenate(
                    [
                        o_all[parity, 4 * half : 4 * half + 4, zh + k].reshape(4 * TOK, DH)
                        for k in range(2)
                    ],
                    axis=1,
                )
                right = jnp.concatenate(
                    [w_all[zh + k, 2 * parity + n] for k in range(2) for n in range(2)], axis=0
                )
                term = jnp.dot(left, right, preferred_element_type=jnp.float32)
                projected = term if projected is None else projected + term

        for g in range(4 * half, 4 * half + 4):
            rows = slice((g % 4) * TOK, (g % 4 + 1) * TOK)
            stream = hid_all[g].astype(jnp.float32) + consts[0, g : g + 1, :] * projected[rows]
            center = jnp.mean(stream, axis=1, keepdims=True)
            apart = stream - center
            spread = jnp.sum(apart * apart, axis=1, keepdims=True)
            scaled = (apart * consts[2, g : g + 1, :]).astype(jnp.bfloat16)
            mixed = lax.dot_general(
                scaled,
                final_buf[...],
                (((1,), (1,)), ((), ())),
                preferred_element_type=jnp.float32,
            )
            message[g, 0 : TOK // 2] = jnp.concatenate(
                [mixed[: TOK // 2], mixed[TOK // 2 :]], axis=1
            )
            both_sums = jnp.concatenate([sums[0, g : g + 1], sums[1, g : g + 1]], axis=1)
            message[g, TOK // 2 :] = jnp.where(
                last_row == 0,
                as_row(center),
                jnp.where(last_row == 1, as_row(spread), both_sums),
            )
        for g in range(4 * half, 4 * half + 4):
            for later in range(2 if g < NQ - 1 else 1):

                @pl.when(queue != g + later)
                def _():
                    remote(
                        message.at[g],
                        received.at[later, queue],
                        send_m.at[later, g],
                        recv_m.at[later, queue],
                        {"queue": g + later, "seq": seq},
                    ).start()

                @pl.when(queue == g + later)
                def _():
                    pltpu.make_async_copy(
                        message.at[g], received.at[later, queue], recv_m.at[later, queue]
                    ).start()

    def velocity_of(later):
        for source in range(NQ):
            wait_bytes(received.at[later, source], recv_m.at[later, source])
        tails = [received[later, source, TOK // 2 :] for source in range(NQ)]
        center = functools.reduce(jnp.add, [tail[0:1] for tail in tails]) / NQ
        spread = functools.reduce(jnp.add, [tail[1:2] for tail in tails])
        mixed = functools.reduce(
            jnp.add, [received[later, source, : TOK // 2] for source in range(NQ)]
        )
        mixed = jnp.concatenate([mixed[:, :LAT], mixed[:, LAT:]], axis=0)
        offset = functools.reduce(jnp.add, [tail[2:3, LAT:] for tail in tails])
        for tail in tails:
            away = tail[0:1] - center
            spread = spread + COLS * (away * away)
            mixed = mixed + as_column(away) * tail[2:3, :LAT]
        return mixed * as_column(1.0 / jnp.sqrt(spread / D + 1e-06)) + offset

    wait_bytes(hid_all.at[pl.ds(0, NQ - 1)], send_h.at[0])
    wait_bytes(act_all.at[pl.ds(0, NQ - 1)], send_h.at[1])
    for array in range(3):
        wait_bytes(q_buf.at[pl.ds(0, 3), pl.ds(0, 5), 0], send_a.at[array])

    @pl.when(xt != x)
    def _():
        wait_bytes(q_buf.at[0, 0, 0], send_a.at[3])

    @pl.when(queue < NQ - 1)
    def _():
        wait_bytes(lat_behind, send_h.at[2])

    for d in range(3):
        wait_bytes(w_all.at[0, 0], send_wy.at[d])
    for side in range(2):
        for array in range(2):
            for n in range(3):
                wait_bytes(k_buf.at[0], send_x.at[array, side, n])
        wait_bytes(q_buf.at[0], send_y.at[side, 0])
        wait_bytes(q_buf.at[0, pl.ds(0, 4)], send_y.at[side, 1])
        for step in range(4):
            wait_bytes(w_all.at[0, pl.ds(0, NY if step < 3 else 2)], send_wz.at[side, step])
    for d in (1, 2, 3):
        for half in range(2):
            wait_bytes(o_part.at[0, 0], send_o.at[half, d - 1])
            wait_bytes(o_all.at[0, 0], send_g.at[half, d - 1])
    wait_bytes(merged.at[pl.ds(0, 7)], send_z.at[0])
    for slot in range(8):
        wait_bytes(o_all.at[0, 0], send_c.at[slot])
    for g in range(NQ):
        for later in range(2 if g < NQ - 1 else 1):

            @pl.when(queue != g + later)
            def _():
                wait_bytes(message.at[0], send_m.at[later, g])

    out_ref[:, 0:LAT] = velocity_of(0)

    @pl.when(queue == 0)
    def _():
        out_ref[:, LAT:] = fresh_buf[...]

    @pl.when(queue > 0)
    def _():
        velocity = velocity_of(1)
        wait_bytes(lat_behind, recv_h.at[2])
        out_ref[:, LAT:] = lat_behind[...] - STRIDE / 1000.0 * velocity


def fused(*operands):
    bf16, f32 = jnp.bfloat16, jnp.float32
    vmem, dma = pltpu.VMEM, pltpu.SemaphoreType.DMA
    in_specs = [pl.BlockSpec(memory_space=pl.ANY)] * 10
    in_specs[5] = pl.BlockSpec(memory_space=pltpu.SMEM)
    return pl.pallas_call(
        fused_kernel,
        out_shape=jax.ShapeDtypeStruct((TOK, 2 * LAT), f32),
        in_specs=in_specs,
        out_specs=pl.BlockSpec(memory_space=pltpu.VMEM),
        scratch_shapes=[
            vmem((NQ, NZ, TOK, DH), bf16),
            vmem((NQ, NZ, TOK, DH), bf16),
            vmem((NY, NQ, 2, TOK, DH), bf16),
            vmem((NQ, NY * ROWS, 256), f32),
            vmem((NQ, NY * ROWS, 128), f32),
            vmem((NY, 2, PART, DH), bf16),
            vmem((NY, 2, PART, DH), bf16),
            vmem((NQ, 2, TOK, DH), bf16),
            vmem((NC, NQ, NZ, TOK, DH), bf16),
            vmem((NQ, TOK, COLS), bf16),
            vmem((NQ, 8, TEMB), f32),
            vmem((NZ, NY, 64, COLS), bf16),
            vmem((3, TEMB, COLS), bf16),
            vmem((LAT, COLS), bf16),
            vmem((TOK, LAT), f32),
            vmem((TOK, LAT), f32),
            vmem((3, NQ, COLS), f32),
            vmem((2, NQ, LAT), f32),
            vmem((NQ, MSG, 128), f32),
            vmem((2, NQ, MSG, 128), f32),
            dma((5,)),
            dma((4,)),
            dma((3,)),
            dma((3,)),
            dma((2, 4)),
            dma((2, 2, 3)),
            dma((2, 2)),
            dma((2, 3)),
            dma((1,)),
            dma((2, 3)),
            dma((8,)),
            dma((2, NQ)),
            dma((2,)),
            dma((2,)),
            dma((1,)),
            dma((3,)),
            dma((1,)),
            dma((2, 4)),
            dma((2, 2, 3)),
            dma((2, 2)),
            dma((2, 3)),
            dma((2,)),
            dma((2, 3)),
            dma((8,)),
            dma((2, NQ)),
        ],
        compiler_params=pltpu.CompilerParams(
            collective_id=0, has_side_effects=True, vmem_limit_bytes=60 * 1024 * 1024
        ),
        name="fused",
    )(*operands)


def body(
    hidden,
    queries,
    keys,
    values,
    timesteps,
    latents,
    fresh_noise,
    out_weight,
    mod_weight,
    final_weight,
):
    result = fused(
        queries[0],
        keys[0],
        values[0],
        hidden[0],
        out_weight,
        timesteps,
        mod_weight,
        final_weight.T,
        latents[0],
        fresh_noise,
    )
    return result[None, :, :LAT], result[None, :, LAT:]


def solution(mesh):
    placed = (
        P("queue", "seq", None),
        P("queue", "seq", None),
        P("queue", "seq", None),
        P("queue", "seq", None),
        P("queue"),
        P("queue", "seq", None),
        P("seq", None),
        P("seq", None),
        P(),
        P(),
    )
    return jax.shard_map(
        body,
        mesh=mesh,
        in_specs=placed,
        out_specs=(P("queue", "seq", None), P("queue", "seq", None)),
        check_vma=False,
    )
```

```python
import functools
import math

import jax
import jax.numpy as jnp
from jax import lax
from jax.experimental import pallas as pl
from jax.experimental.pallas import tpu as pltpu
from jax.sharding import PartitionSpec as P

D = 3072
H = 16
DH = 128
TEMB = 256
STRIDE = 125
NX, NC, NY, NZ = 4, 2, 4, 8
NQ = NX * NC
TOK = 48
COLS = D // NQ
LAT = 64
ROWS = 2 * TOK
PART = 4 * ROWS + 16
MSG = TOK // 2 + 8
SCALE = DH**-0.5 * math.log2(math.e)
MESH = pl.DeviceIdType.MESH


def place(x, c, y, z):
    return {"queue": x * NC + c, "seq": z * NY + y}


def remote(src, dst, send_sem, recv_sem, device):
    return pltpu.make_async_remote_copy(
        src_ref=src,
        dst_ref=dst,
        send_sem=send_sem,
        recv_sem=recv_sem,
        device_id=device,
        device_id_type=MESH,
    )


def wait_bytes(ref, sem):
    pltpu.make_async_copy(ref, ref, sem).wait()


def attend(tasks, q_buf, acc, peak):
    scores = [
        lax.dot_general(
            q_buf[:, i].reshape(NY * ROWS, DH),
            keys,
            (((1,), (1,)), ((), ())),
            preferred_element_type=jnp.float32,
        )
        for i, keys, _ in tasks
    ]
    for (i, _, values), block in zip(tasks, scores):
        extended = jnp.concatenate([values, jnp.ones_like(values)], axis=1)
        weights, factors = [], []
        for part in range(3):
            rows = slice(part * 128, part * 128 + 128)
            piece = block[rows] * SCALE
            old = peak[i, rows, :]
            new = jnp.maximum(old, jnp.max(piece, axis=1, keepdims=True))
            peak[i, rows, :] = new
            factors.append(jnp.exp2(old - new))
            wide = jnp.concatenate([new] * (piece.shape[1] // 128), axis=1)
            weights.append(jnp.exp2(piece - wide).astype(jnp.bfloat16))
        mixed = jnp.dot(
            jnp.concatenate(weights, axis=0), extended, preferred_element_type=jnp.float32
        )
        for part, factor in enumerate(factors):
            rows = slice(part * 128, part * 128 + 128)
            acc[i, rows, :] = (
                acc[i, rows, :] * jnp.concatenate([factor, factor], axis=1) + mixed[rows]
            )


def fused_kernel(
    q_ref,
    k_ref,
    v_ref,
    hid_ref,
    w_ref,
    step_ref,
    mod_ref,
    final_ref,
    lat_ref,
    fresh_ref,
    out_ref,
    k_buf,
    v_buf,
    q_buf,
    acc,
    peak,
    o_part,
    o_recv,
    merged,
    o_all,
    hid_all,
    act_all,
    w_all,
    mod_buf,
    final_buf,
    lat_behind,
    fresh_buf,
    consts,
    sums,
    message,
    received,
    load_sem,
    send_a,
    send_h,
    send_wy,
    send_wz,
    send_x,
    send_y,
    send_o,
    send_z,
    send_g,
    send_c,
    send_m,
    recv_k,
    recv_v,
    recv_q,
    recv_h,
    recv_wy,
    recv_wz,
    recv_x,
    recv_y,
    recv_o,
    recv_z,
    recv_g,
    recv_c,
    recv_m,
):
    queue = lax.axis_index("queue")
    seq = lax.axis_index("seq")
    x, c = queue // NC, queue % NC
    z, y = seq // NY, seq % NY
    xl, xr, x2 = (x + NX - 1) % NX, (x + 1) % NX, (x + 2) % NX
    yl, yr, y2 = (y + NY - 1) % NY, (y + 1) % NY, (y + 2) % NY
    zl, zr = (z + NZ - 1) % NZ, (z + 1) % NZ
    zk = z // 4
    xt = (z + queue) % NX
    own_head = 2 * z + c
    barrier = pltpu.get_barrier_semaphore()

    queues = [(queue + d) % NQ for d in range(NQ)]
    seqs = [(seq + d * NY) % (NY * NZ) for d in range(NZ)]
    for d, q2 in enumerate(queues):
        for e, s2 in enumerate(seqs):
            if d or e:
                pl.semaphore_signal(
                    barrier, inc=1, device_id={"queue": q2, "seq": s2}, device_id_type=MESH
                )
    for d in (1, 2, 3):
        pl.semaphore_signal(
            barrier, inc=1, device_id=place(x, c, (y + d) % NY, z), device_id_type=MESH
        )

    def own_columns(part):
        return pl.ds(pl.multiple_of(part * D + queue * COLS, 128), COLS)

    loads = [
        pltpu.make_async_copy(mod_ref.at[:, own_columns(n)], mod_buf.at[n], load_sem.at[n])
        for n in range(3)
    ]
    loads.append(pltpu.make_async_copy(final_ref.at[:, own_columns(0)], final_buf, load_sem.at[3]))
    loads.append(pltpu.make_async_copy(fresh_ref, fresh_buf, load_sem.at[4]))
    for load in loads:
        load.start()

    pl.semaphore_wait(barrier, 66)

    def columns(ref, head):
        return ref.at[:, pl.ds(pl.multiple_of(head * DH, DH), DH)]

    def by_head(array, ref, target, sem, xs):
        for n in range(1, 16):
            zt, ct = zs[n // 2], cs[n % 2]
            remote(
                columns(ref, 2 * zt + ct),
                target,
                send_a.at[array],
                sem,
                {"queue": xs * NC + ct, "seq": seqs[n // 2]},
            ).start()

    zs = [(z + d) % NZ for d in range(NZ)]
    cs = [c, 1 - c]
    by_head(1, q_ref, q_buf.at[y, queue, zk], recv_q.at[0], xt)

    @pl.when(xt != x)
    def _():
        remote(
            columns(q_ref, own_head),
            q_buf.at[y, queue, zk],
            send_a.at[3],
            recv_q.at[0],
            place(xt, c, y, z),
        ).start()

    @pl.when(xt == x)
    def _():
        pltpu.make_async_copy(
            columns(q_ref, own_head), q_buf.at[y, queue, zk], recv_q.at[0]
        ).start()

    by_head(0, k_ref, k_buf.at[queue, z], recv_k.at[c], x)
    pltpu.make_async_copy(columns(k_ref, own_head), k_buf.at[queue, z], recv_k.at[c]).start()
    for d in (1, 2, 3):
        remote(
            w_ref.at[:, own_columns(0)],
            w_all.at[z, y],
            send_wy.at[d - 1],
            recv_wy.at[0],
            place(x, c, (y + d) % NY, z),
        ).start()
    pltpu.make_async_copy(w_ref.at[:, own_columns(0)], w_all.at[z, y], recv_wy.at[0]).start()

    halfway = TEMB // 2
    index = lax.broadcasted_iota(jnp.int32, (8, halfway), 1).astype(jnp.float32)
    angles = step_ref[0].astype(jnp.float32) * jnp.exp(-math.log(10000.0) * index / halfway)
    embed = jnp.concatenate([jnp.cos(angles), jnp.sin(angles)], axis=1)
    act_all[queue] = embed / (1.0 + jnp.exp(-embed))

    for to in queues[1:]:
        remote(
            act_all.at[queue],
            act_all.at[queue],
            send_h.at[1],
            recv_h.at[1],
            {"queue": to, "seq": seq},
        ).start()

    @pl.when(queue < NQ - 1)
    def _():
        remote(
            lat_ref,
            lat_behind,
            send_h.at[2],
            recv_h.at[2],
            {"queue": (queue + 1) % NQ, "seq": seq},
        ).start()

    acc[...] = jnp.zeros_like(acc)
    peak[...] = jnp.full_like(peak, -1e30)

    def along_x(array, ref):
        for n in range(2):
            for side, to in ((0, xr), (1, xl)):
                blk = n if side == 0 else 1 - n
                block = ref.at[2 * x + blk]
                remote(
                    block,
                    block,
                    send_x.at[array, side, blk],
                    recv_x.at[array, side, blk],
                    place(to, c, y, z),
                ).start()

    def relay_x(array, ref):
        for side, source, to in ((0, xl, xr), (1, xr, xl)):
            block = ref.at[2 * source + side]
            wait_bytes(block, recv_x.at[array, side, side])
            remote(
                block,
                block,
                send_x.at[array, side, 2],
                recv_x.at[array, side, 2],
                place(to, c, y, z),
            ).start()

    wait_bytes(q_buf.at[y], recv_q.at[0])
    for side, to in ((0, yr), (1, yl)):
        remote(
            q_buf.at[y], q_buf.at[y], send_y.at[side, 0], recv_y.at[side, 0], place(x, c, to, z)
        ).start()

    by_head(2, v_ref, v_buf.at[queue, z], recv_v.at[c], x)
    pltpu.make_async_copy(columns(v_ref, own_head), v_buf.at[queue, z], recv_v.at[c]).start()

    for blk in range(2):
        wait_bytes(k_buf.at[2 * x + blk], recv_k.at[blk])
    along_x(0, k_buf)

    for load in loads:
        load.wait()
    wait_bytes(act_all.at[pl.ds(0, NQ - 1)], recv_h.at[1])
    act = act_all[:, 0, :].astype(jnp.bfloat16)
    for n in range(3):
        consts[n] = jnp.dot(act, mod_buf[n], preferred_element_type=jnp.float32)
    consts[2] = 1.0 + consts[2]
    final32 = final_buf[...].astype(jnp.float32)
    for n in range(2):
        sums[n] = lax.dot_general(
            consts[2 - n],
            final32,
            (((1,), (1,)), ((), ())),
            preferred_element_type=jnp.float32,
            precision=lax.Precision.HIGHEST,
        )

    for side, source, to in ((0, yl, yr), (1, yr, yl)):
        wait_bytes(q_buf.at[source], recv_y.at[side, 0])
        slab = q_buf.at[source, pl.ds(4 * side, 4)]
        remote(
            slab, slab, send_y.at[side, 1], recv_y.at[side, 1], place(x, c, to, z)
        ).start()

    for blk in range(2):
        wait_bytes(v_buf.at[2 * x + blk], recv_v.at[blk])
    along_x(1, v_buf)
    relay_x(0, k_buf)

    def send_hidden(d, carry):
        to = (queue + d) % NQ
        remote(
            hid_ref.at[:, pl.ds(pl.multiple_of(to * COLS, 128), COLS)],
            hid_all.at[queue],
            send_h.at[0],
            recv_h.at[0],
            {"queue": to, "seq": seq},
        ).start()
        return carry

    def ring_z(step):
        for side, to in ((0, zr), (1, zl)):
            back = NZ - step if side == 0 else step
            rows = pl.ds(0, NY) if step < 3 else pl.ds(2 * side, 2)
            chunk = w_all.at[(z + back) % NZ]
            if step:
                wait_bytes(chunk, recv_wz.at[side, step - 1])
            chunk = w_all.at[(z + back) % NZ, rows]
            remote(
                chunk,
                chunk,
                send_wz.at[side, step],
                recv_wz.at[side, step],
                place(x, c, y, to),
            ).start()

    wait_bytes(w_all.at[z], recv_wy.at[0])
    ring_z(0)
    for side in range(2):
        wait_bytes(q_buf.at[y2, pl.ds(4 * side, 4)], recv_y.at[side, 1])

    lane = lax.broadcasted_iota(jnp.int32, (ROWS, 128), 1)
    row = lax.broadcasted_iota(jnp.int32, (ROWS, 128), 0)
    diagonal = lane == row
    stat_row = lax.broadcasted_iota(jnp.int32, (16, 128), 0)

    def finish(half):
        vectors = [[] for _ in range(NY)]
        for k in range(4):
            g = 4 * half + k
            total = acc[g, :, 128:]
            out = (acc[g, :, :128] / total).astype(jnp.bfloat16)
            level = peak[g] + jnp.log2(total)
            for part in range(NY):
                rows = slice(part * ROWS, (part + 1) * ROWS)
                vector = jnp.sum(jnp.where(diagonal, level[rows], 0.0), axis=0, keepdims=True)
                high = vector.astype(jnp.bfloat16).astype(jnp.float32)
                middle = (vector - high).astype(jnp.bfloat16).astype(jnp.float32)
                vectors[part] += [high, middle, vector - high - middle]
                o_part[part, half, k * ROWS : (k + 1) * ROWS] = out[rows]
        for part in range(NY):
            stats = jnp.zeros((16, 128), jnp.float32)
            for n, vector in enumerate(vectors[part]):
                stats = jnp.where(stat_row == n, vector, stats)
            o_part[part, half, 4 * ROWS :] = stats.astype(jnp.bfloat16)

    def partial_copy(half, d):
        to = (y + d) % NY
        return remote(
            o_part.at[to, half],
            o_recv.at[y, half],
            send_o.at[half, d - 1],
            recv_o.at[half, d - 1],
            place(x, c, to, z),
        )

    key_rows = NZ * TOK

    def stage(st, carry):
        p = (x + st + st // 2 - 2 * (st // 3)) % NX

        @pl.when(st == 1)
        def _():
            relay_x(1, v_buf)
            for ref, array in ((k_buf, 0), (v_buf, 1)):
                wait_bytes(ref.at[2 * xr], recv_x.at[array, 1, 0])

        @pl.when(st == 2)
        def _():
            ring_z(1)
            for ref, array in ((k_buf, 0), (v_buf, 1)):
                wait_bytes(ref.at[2 * xl + 1], recv_x.at[array, 0, 1])

        @pl.when(st == 3)
        def _():
            for ref, array in ((k_buf, 0), (v_buf, 1)):
                for side in range(2):
                    wait_bytes(ref.at[2 * x2 + side], recv_x.at[array, side, 2])
            lax.fori_loop(1, NQ, send_hidden, 0)
            pltpu.make_async_copy(
                hid_ref.at[:, own_columns(0)], hid_all.at[queue], recv_h.at[0]
            ).start()

        high, odd = p // 2, p % 2

        def both(j, carry):
            keys = k_buf[pl.ds(2 * p, 2)].reshape(2 * key_rows, DH)
            values = v_buf[pl.ds(2 * p, 2)].reshape(2 * key_rows, DH)
            attend([(2 * j, keys, values), (2 * j + 1, keys, values)], q_buf, acc, peak)
            return carry

        def halves(half, carry):
            same = 1 - (high - half) * (high - half)
            count = 2 * high * (1 - half) + odd * same
            lax.fori_loop(2 * half, 2 * half + count, both, 0)

            @pl.when(high == half)
            def _():
                keys = k_buf[pl.ds(2 * p, 2)].reshape(2 * key_rows, DH)
                values = v_buf[pl.ds(2 * p, 2)].reshape(2 * key_rows, DH)
                attend(
                    [
                        (2 * p, keys, values),
                        (2 * p + 1, keys[key_rows:], values[key_rows:]),
                    ],
                    q_buf,
                    acc,
                    peak,
                )

            @pl.when(st == 3)
            def _():
                finish(half)
                for d in (2, 1, 3):
                    partial_copy(half, d).start()

                @pl.when(half == 0)
                def _():
                    ring_z(2)

            return carry

        return lax.fori_loop(0, 2, halves, carry)

    lax.fori_loop(0, 4, stage, 0)
    ring_z(3)

    def column(vector):
        return jnp.sum(
            jnp.where(diagonal, jnp.broadcast_to(vector, (ROWS, 128)), 0.0),
            axis=1,
            keepdims=True,
        )

    def merge(half):
        refs = [o_part.at[y, half]] + [o_recv.at[(y + d) % NY, half] for d in (1, 2, 3)]
        stats = [ref[4 * ROWS :].astype(jnp.float32) for ref in refs]
        for k in range(4):
            g = 4 * half + k
            levels = [
                column(stat[3 * k : 3 * k + 1] + stat[3 * k + 1 : 3 * k + 2] + stat[3 * k + 2 : 3 * k + 3])
                for stat in stats
            ]
            top = functools.reduce(jnp.maximum, levels)
            shares = [jnp.exp2(level - top) for level in levels]
            total = functools.reduce(jnp.add, shares)
            mixed = functools.reduce(
                jnp.add,
                [
                    share * ref[k * ROWS : (k + 1) * ROWS].astype(jnp.float32)
                    for share, ref in zip(shares, refs)
                ],
            )
            merged[g] = (mixed / total).astype(jnp.bfloat16).reshape(2, TOK, DH)
        for k in range(4):
            g = 4 * half + k
            for n in range(2):
                zt = (x + 8 - g) % 4 + 4 * n

                @pl.when(zt != z)
                def _():
                    remote(
                        merged.at[g, n],
                        o_all.at[c, g, z],
                        send_z.at[0],
                        recv_z.at[half],
                        place(x, c, y, zt),
                    ).start()

                @pl.when(zt == z)
                def _():
                    pltpu.make_async_copy(
                        merged.at[g, n], o_all.at[c, g, z], recv_z.at[half]
                    ).start()

    def first(xs):
        return (xs + 8 - z) % 4

    def across(g, slot):
        return remote(
            o_all.at[c, g],
            o_all.at[c, g],
            send_c.at[slot],
            recv_c.at[slot],
            place(x, 1 - c, y, z),
        )

    for half in range(2):
        for d in (1, 3, 2):
            wait_bytes(o_recv.at[(y + NY - d) % NY, half], recv_o.at[half, d - 1])
        merge(half)
    for half in range(2):
        g = first(x) + 4 * half
        wait_bytes(o_all.at[c, g], recv_z.at[half])
        for d in (2, 1, 3):
            remote(
                o_all.at[c, g],
                o_all.at[c, g],
                send_g.at[half, d - 1],
                recv_g.at[half, d - 1],
                place((x + d) % NX, c, y, z),
            ).start()
        across(g, 4 * half).start()

    wait_bytes(hid_all, recv_h.at[0])
    for side in range(2):
        wait_bytes(w_all.at[(z + 4) % NZ, pl.ds(2 * side, 2)], recv_wz.at[side, 3])

    token_lane = lax.broadcasted_iota(jnp.int32, (TOK, 128), 1)
    token_row = lax.broadcasted_iota(jnp.int32, (TOK, 128), 0)
    token_diagonal = token_lane == token_row
    last_row = lax.broadcasted_iota(jnp.int32, (8, 128), 0)

    def as_row(vector):
        return jnp.sum(
            jnp.where(token_diagonal, jnp.broadcast_to(vector, (TOK, 128)), 0.0),
            axis=0,
            keepdims=True,
        )

    def as_column(vector):
        return jnp.sum(
            jnp.where(token_diagonal, jnp.broadcast_to(vector, (TOK, 128)), 0.0),
            axis=1,
            keepdims=True,
        )

    for half in range(2):
        for d in (1, 3, 2):
            g = first((x + NX - d) % NX) + 4 * half
            wait_bytes(o_all.at[c, g], recv_g.at[half, d - 1])
            across(g, 4 * half + d).start()
        projected = None
        for parity in (c, 1 - c):
            if projected is not None:
                for d in range(NX):
                    g = first((x + NX - d) % NX) + 4 * half
                    wait_bytes(o_all.at[parity, g], recv_c.at[4 * half + d])
            for zh in range(0, NZ, 2):
                left = jnp.concatenate(
                    [
                        o_all[parity, 4 * half : 4 * half + 4, zh + k].reshape(4 * TOK, DH)
                        for k in range(2)
                    ],
                    axis=1,
                )
                right = jnp.concatenate(
                    [w_all[zh + k, 2 * parity + n] for k in range(2) for n in range(2)], axis=0
                )
                term = jnp.dot(left, right, preferred_element_type=jnp.float32)
                projected = term if projected is None else projected + term

        for g in range(4 * half, 4 * half + 4):
            rows = slice((g % 4) * TOK, (g % 4 + 1) * TOK)
            stream = hid_all[g].astype(jnp.float32) + consts[0, g : g + 1, :] * projected[rows]
            center = jnp.mean(stream, axis=1, keepdims=True)
            apart = stream - center
            spread = jnp.sum(apart * apart, axis=1, keepdims=True)
            scaled = (apart * consts[2, g : g + 1, :]).astype(jnp.bfloat16)
            mixed = lax.dot_general(
                scaled,
                final_buf[...],
                (((1,), (1,)), ((), ())),
                preferred_element_type=jnp.float32,
            )
            message[g, 0 : TOK // 2] = jnp.concatenate(
                [mixed[: TOK // 2], mixed[TOK // 2 :]], axis=1
            )
            both_sums = jnp.concatenate([sums[0, g : g + 1], sums[1, g : g + 1]], axis=1)
            message[g, TOK // 2 :] = jnp.where(
                last_row == 0,
                as_row(center),
                jnp.where(last_row == 1, as_row(spread), both_sums),
            )
        for g in range(4 * half, 4 * half + 4):
            for later in range(2 if g < NQ - 1 else 1):

                @pl.when(queue != g + later)
                def _():
                    remote(
                        message.at[g],
                        received.at[later, queue],
                        send_m.at[later, g],
                        recv_m.at[later, queue],
                        {"queue": g + later, "seq": seq},
                    ).start()

                @pl.when(queue == g + later)
                def _():
                    pltpu.make_async_copy(
                        message.at[g], received.at[later, queue], recv_m.at[later, queue]
                    ).start()

    def velocity_of(later):
        for source in range(NQ):
            wait_bytes(received.at[later, source], recv_m.at[later, source])
        tails = [received[later, source, TOK // 2 :] for source in range(NQ)]
        center = functools.reduce(jnp.add, [tail[0:1] for tail in tails]) / NQ
        spread = functools.reduce(jnp.add, [tail[1:2] for tail in tails])
        mixed = functools.reduce(
            jnp.add, [received[later, source, : TOK // 2] for source in range(NQ)]
        )
        mixed = jnp.concatenate([mixed[:, :LAT], mixed[:, LAT:]], axis=0)
        offset = functools.reduce(jnp.add, [tail[2:3, LAT:] for tail in tails])
        for tail in tails:
            away = tail[0:1] - center
            spread = spread + COLS * (away * away)
            mixed = mixed + as_column(away) * tail[2:3, :LAT]
        return mixed * as_column(1.0 / jnp.sqrt(spread / D + 1e-06)) + offset

    wait_bytes(hid_all.at[pl.ds(0, NQ - 1)], send_h.at[0])
    wait_bytes(act_all.at[pl.ds(0, NQ - 1)], send_h.at[1])
    for array in range(3):
        wait_bytes(q_buf.at[pl.ds(0, 3), pl.ds(0, 5), 0], send_a.at[array])

    @pl.when(xt != x)
    def _():
        wait_bytes(q_buf.at[0, 0, 0], send_a.at[3])

    @pl.when(queue < NQ - 1)
    def _():
        wait_bytes(lat_behind, send_h.at[2])

    for d in range(3):
        wait_bytes(w_all.at[0, 0], send_wy.at[d])
    for side in range(2):
        for array in range(2):
            for n in range(3):
                wait_bytes(k_buf.at[0], send_x.at[array, side, n])
        wait_bytes(q_buf.at[0], send_y.at[side, 0])
        wait_bytes(q_buf.at[0, pl.ds(0, 4)], send_y.at[side, 1])
        for step in range(4):
            wait_bytes(w_all.at[0, pl.ds(0, NY if step < 3 else 2)], send_wz.at[side, step])
    for d in (1, 2, 3):
        for half in range(2):
            wait_bytes(o_part.at[0, 0], send_o.at[half, d - 1])
            wait_bytes(o_all.at[0, 0], send_g.at[half, d - 1])
    wait_bytes(merged.at[pl.ds(0, 7)], send_z.at[0])
    for slot in range(8):
        wait_bytes(o_all.at[0, 0], send_c.at[slot])
    for g in range(NQ):
        for later in range(2 if g < NQ - 1 else 1):

            @pl.when(queue != g + later)
            def _():
                wait_bytes(message.at[0], send_m.at[later, g])

    out_ref[:, 0:LAT] = velocity_of(0)

    @pl.when(queue == 0)
    def _():
        out_ref[:, LAT:] = fresh_buf[...]

    @pl.when(queue > 0)
    def _():
        velocity = velocity_of(1)
        wait_bytes(lat_behind, recv_h.at[2])
        out_ref[:, LAT:] = lat_behind[...] - STRIDE / 1000.0 * velocity


def fused(*operands):
    bf16, f32 = jnp.bfloat16, jnp.float32
    vmem, dma = pltpu.VMEM, pltpu.SemaphoreType.DMA
    in_specs = [pl.BlockSpec(memory_space=pl.ANY)] * 10
    in_specs[5] = pl.BlockSpec(memory_space=pltpu.SMEM)
    return pl.pallas_call(
        fused_kernel,
        out_shape=pltpu.VMEM((TOK, 2 * LAT), f32),
        in_specs=in_specs,
        out_specs=pl.BlockSpec(memory_space=pltpu.VMEM),
        scratch_shapes=[
            vmem((NQ, NZ, TOK, DH), bf16),
            vmem((NQ, NZ, TOK, DH), bf16),
            vmem((NY, NQ, 2, TOK, DH), bf16),
            vmem((NQ, NY * ROWS, 256), f32),
            vmem((NQ, NY * ROWS, 128), f32),
            vmem((NY, 2, PART, DH), bf16),
            vmem((NY, 2, PART, DH), bf16),
            vmem((NQ, 2, TOK, DH), bf16),
            vmem((NC, NQ, NZ, TOK, DH), bf16),
            vmem((NQ, TOK, COLS), bf16),
            vmem((NQ, 8, TEMB), f32),
            vmem((NZ, NY, 64, COLS), bf16),
            vmem((3, TEMB, COLS), bf16),
            vmem((LAT, COLS), bf16),
            vmem((TOK, LAT), f32),
            vmem((TOK, LAT), f32),
            vmem((3, NQ, COLS), f32),
            vmem((2, NQ, LAT), f32),
            vmem((NQ, MSG, 128), f32),
            vmem((2, NQ, MSG, 128), f32),
            dma((5,)),
            dma((4,)),
            dma((3,)),
            dma((3,)),
            dma((2, 4)),
            dma((2, 2, 3)),
            dma((2, 2)),
            dma((2, 3)),
            dma((1,)),
            dma((2, 3)),
            dma((8,)),
            dma((2, NQ)),
            dma((2,)),
            dma((2,)),
            dma((1,)),
            dma((3,)),
            dma((1,)),
            dma((2, 4)),
            dma((2, 2, 3)),
            dma((2, 2)),
            dma((2, 3)),
            dma((2,)),
            dma((2, 3)),
            dma((8,)),
            dma((2, NQ)),
        ],
        compiler_params=pltpu.CompilerParams(
            collective_id=0, has_side_effects=True, vmem_limit_bytes=60 * 1024 * 1024
        ),
        name="fused",
    )(*operands)


def body(
    hidden,
    queries,
    keys,
    values,
    timesteps,
    latents,
    fresh_noise,
    out_weight,
    mod_weight,
    final_weight,
):
    result = fused(
        queries[0],
        keys[0],
        values[0],
        hidden[0],
        out_weight,
        timesteps,
        mod_weight,
        final_weight.T,
        latents[0],
        fresh_noise,
    )
    return result[None, :, :LAT], result[None, :, LAT:]


def solution(mesh):
    placed = (
        P("queue", "seq", None),
        P("queue", "seq", None),
        P("queue", "seq", None),
        P("queue", "seq", None),
        P("queue"),
        P("queue", "seq", None),
        P("seq", None),
        P("seq", None),
        P(),
        P(),
    )
    return jax.shard_map(
        body,
        mesh=mesh,
        in_specs=placed,
        out_specs=(P("queue", "seq", None), P("queue", "seq", None)),
        check_vma=False,
    )
```

```python
import functools
import math

import jax
import jax.numpy as jnp
from jax import lax
from jax.experimental import pallas as pl
from jax.experimental.pallas import tpu as pltpu
from jax.sharding import PartitionSpec as P

D = 3072
H = 16
DH = 128
TEMB = 256
STRIDE = 125
NX, NC, NY, NZ = 4, 2, 4, 8
NQ = NX * NC
TOK = 48
COLS = D // NQ
LAT = 64
ROWS = 2 * TOK
PART = 4 * ROWS + 16
MSG = TOK // 2 + 8
SCALE = DH**-0.5 * math.log2(math.e)
MESH = pl.DeviceIdType.MESH


def place(x, c, y, z):
    return {"queue": x * NC + c, "seq": z * NY + y}


def remote(src, dst, send_sem, recv_sem, device):
    return pltpu.make_async_remote_copy(
        src_ref=src,
        dst_ref=dst,
        send_sem=send_sem,
        recv_sem=recv_sem,
        device_id=device,
        device_id_type=MESH,
    )


def wait_bytes(ref, sem):
    pltpu.make_async_copy(ref, ref, sem).wait()


def attend(tasks, q_buf, acc, peak):
    scores = [
        lax.dot_general(
            q_buf[:, i].reshape(NY * ROWS, DH),
            keys,
            (((1,), (1,)), ((), ())),
            preferred_element_type=jnp.float32,
        )
        for i, keys, _ in tasks
    ]
    for (i, _, values), block in zip(tasks, scores):
        extended = jnp.concatenate([values, jnp.ones_like(values)], axis=1)
        weights, factors = [], []
        for part in range(3):
            rows = slice(part * 128, part * 128 + 128)
            piece = block[rows] * SCALE
            old = peak[i, rows, :]
            new = jnp.maximum(old, jnp.max(piece, axis=1, keepdims=True))
            peak[i, rows, :] = new
            factors.append(jnp.exp2(old - new))
            wide = jnp.concatenate([new] * (piece.shape[1] // 128), axis=1)
            weights.append(jnp.exp2(piece - wide).astype(jnp.bfloat16))
        mixed = jnp.dot(
            jnp.concatenate(weights, axis=0), extended, preferred_element_type=jnp.float32
        )
        for part, factor in enumerate(factors):
            rows = slice(part * 128, part * 128 + 128)
            acc[i, rows, :] = (
                acc[i, rows, :] * jnp.concatenate([factor, factor], axis=1) + mixed[rows]
            )


def fused_kernel(
    q_ref,
    k_ref,
    v_ref,
    hid_ref,
    w_ref,
    step_ref,
    mod_ref,
    final_ref,
    lat_ref,
    fresh_ref,
    out_ref,
    k_buf,
    v_buf,
    q_buf,
    acc,
    peak,
    o_part,
    o_recv,
    merged,
    o_all,
    hid_all,
    act_all,
    w_all,
    mod_buf,
    final_buf,
    lat_behind,
    fresh_buf,
    consts,
    sums,
    message,
    received,
    load_sem,
    send_a,
    send_h,
    send_wy,
    send_wz,
    send_x,
    send_y,
    send_o,
    send_z,
    send_g,
    send_c,
    send_m,
    recv_k,
    recv_v,
    recv_q,
    recv_h,
    recv_wy,
    recv_wz,
    recv_x,
    recv_y,
    recv_o,
    recv_z,
    recv_g,
    recv_c,
    recv_m,
):
    queue = lax.axis_index("queue")
    seq = lax.axis_index("seq")
    x, c = queue // NC, queue % NC
    z, y = seq // NY, seq % NY
    xl, xr, x2 = (x + NX - 1) % NX, (x + 1) % NX, (x + 2) % NX
    yl, yr, y2 = (y + NY - 1) % NY, (y + 1) % NY, (y + 2) % NY
    zl, zr = (z + NZ - 1) % NZ, (z + 1) % NZ
    zk = z // 4
    xt = (z + queue) % NX
    own_head = 2 * z + c
    barrier = pltpu.get_barrier_semaphore()

    queues = [(queue + d) % NQ for d in range(NQ)]
    seqs = [(seq + d * NY) % (NY * NZ) for d in range(NZ)]
    for d, q2 in enumerate(queues):
        for e, s2 in enumerate(seqs):
            if d or e:
                pl.semaphore_signal(
                    barrier, inc=1, device_id={"queue": q2, "seq": s2}, device_id_type=MESH
                )
    for d in (1, 2, 3):
        pl.semaphore_signal(
            barrier, inc=1, device_id=place(x, c, (y + d) % NY, z), device_id_type=MESH
        )

    def own_columns(part):
        return pl.ds(pl.multiple_of(part * D + queue * COLS, 128), COLS)

    loads = [
        pltpu.make_async_copy(mod_ref.at[:, own_columns(n)], mod_buf.at[n], load_sem.at[n])
        for n in range(3)
    ]
    loads.append(pltpu.make_async_copy(final_ref.at[:, own_columns(0)], final_buf, load_sem.at[3]))
    loads.append(pltpu.make_async_copy(fresh_ref, fresh_buf, load_sem.at[4]))
    for load in loads:
        load.start()

    pl.semaphore_wait(barrier, 66)

    def columns(ref, head):
        return ref.at[:, pl.ds(pl.multiple_of(head * DH, DH), DH)]

    def by_head(array, ref, target, sem, xs):
        for n in range(1, 16):
            zt, ct = zs[n // 2], cs[n % 2]
            remote(
                columns(ref, 2 * zt + ct),
                target,
                send_a.at[array],
                sem,
                {"queue": xs * NC + ct, "seq": seqs[n // 2]},
            ).start()

    zs = [(z + d) % NZ for d in range(NZ)]
    cs = [c, 1 - c]
    by_head(1, q_ref, q_buf.at[y, queue, zk], recv_q.at[0], xt)

    @pl.when(xt != x)
    def _():
        remote(
            columns(q_ref, own_head),
            q_buf.at[y, queue, zk],
            send_a.at[3],
            recv_q.at[0],
            place(xt, c, y, z),
        ).start()

    @pl.when(xt == x)
    def _():
        pltpu.make_async_copy(
            columns(q_ref, own_head), q_buf.at[y, queue, zk], recv_q.at[0]
        ).start()

    by_head(0, k_ref, k_buf.at[queue, z], recv_k.at[c], x)
    pltpu.make_async_copy(columns(k_ref, own_head), k_buf.at[queue, z], recv_k.at[c]).start()
    for d in (1, 2, 3):
        remote(
            w_ref.at[:, own_columns(0)],
            w_all.at[z, y],
            send_wy.at[d - 1],
            recv_wy.at[0],
            place(x, c, (y + d) % NY, z),
        ).start()
    pltpu.make_async_copy(w_ref.at[:, own_columns(0)], w_all.at[z, y], recv_wy.at[0]).start()

    halfway = TEMB // 2
    index = lax.broadcasted_iota(jnp.int32, (8, halfway), 1).astype(jnp.float32)
    angles = step_ref[0].astype(jnp.float32) * jnp.exp(-math.log(10000.0) * index / halfway)
    embed = jnp.concatenate([jnp.cos(angles), jnp.sin(angles)], axis=1)
    act_all[queue] = embed / (1.0 + jnp.exp(-embed))

    for to in queues[1:]:
        remote(
            act_all.at[queue],
            act_all.at[queue],
            send_h.at[1],
            recv_h.at[1],
            {"queue": to, "seq": seq},
        ).start()

    @pl.when(queue < NQ - 1)
    def _():
        remote(
            lat_ref,
            lat_behind,
            send_h.at[2],
            recv_h.at[2],
            {"queue": (queue + 1) % NQ, "seq": seq},
        ).start()

    acc[...] = jnp.zeros_like(acc)
    peak[...] = jnp.full_like(peak, -1e30)

    def along_x(array, ref):
        for n in range(2):
            for side, to in ((0, xr), (1, xl)):
                blk = n if side == 0 else 1 - n
                block = ref.at[2 * x + blk]
                remote(
                    block,
                    block,
                    send_x.at[array, side, blk],
                    recv_x.at[array, side, blk],
                    place(to, c, y, z),
                ).start()

    def relay_x(array, ref):
        for side, source, to in ((0, xl, xr), (1, xr, xl)):
            block = ref.at[2 * source + side]
            wait_bytes(block, recv_x.at[array, side, side])
            remote(
                block,
                block,
                send_x.at[array, side, 2],
                recv_x.at[array, side, 2],
                place(to, c, y, z),
            ).start()

    wait_bytes(q_buf.at[y], recv_q.at[0])
    for n in range(2):
        for side, to in ((0, yr), (1, yl)):
            part = n if side == 0 else 1 - n
            slab = q_buf.at[y, pl.ds(4 * part, 4)]
            remote(
                slab, slab, send_y.at[side, part], recv_y.at[side, part], place(x, c, to, z)
            ).start()

    by_head(2, v_ref, v_buf.at[queue, z], recv_v.at[c], x)
    pltpu.make_async_copy(columns(v_ref, own_head), v_buf.at[queue, z], recv_v.at[c]).start()

    for blk in range(2):
        wait_bytes(k_buf.at[2 * x + blk], recv_k.at[blk])
    along_x(0, k_buf)

    for load in loads:
        load.wait()
    wait_bytes(act_all.at[pl.ds(0, NQ - 1)], recv_h.at[1])
    act = act_all[:, 0, :].astype(jnp.bfloat16)
    for n in range(3):
        consts[n] = jnp.dot(act, mod_buf[n], preferred_element_type=jnp.float32)
    consts[2] = 1.0 + consts[2]
    final32 = final_buf[...].astype(jnp.float32)
    for n in range(2):
        sums[n] = lax.dot_general(
            consts[2 - n],
            final32,
            (((1,), (1,)), ((), ())),
            preferred_element_type=jnp.float32,
            precision=lax.Precision.HIGHEST,
        )

    for side, source, to in ((0, yl, yr), (1, yr, yl)):
        slab = q_buf.at[source, pl.ds(4 * side, 4)]
        wait_bytes(slab, recv_y.at[side, side])
        remote(
            slab, slab, send_y.at[side, 2], recv_y.at[side, 2], place(x, c, to, z)
        ).start()

    for blk in range(2):
        wait_bytes(v_buf.at[2 * x + blk], recv_v.at[blk])
    along_x(1, v_buf)
    relay_x(0, k_buf)

    def send_hidden(d, carry):
        to = (queue + d) % NQ
        remote(
            hid_ref.at[:, pl.ds(pl.multiple_of(to * COLS, 128), COLS)],
            hid_all.at[queue],
            send_h.at[0],
            recv_h.at[0],
            {"queue": to, "seq": seq},
        ).start()
        return carry

    def ring_z(step):
        for side, to in ((0, zr), (1, zl)):
            back = NZ - step if side == 0 else step
            rows = pl.ds(0, NY) if step < 3 else pl.ds(2 * side, 2)
            chunk = w_all.at[(z + back) % NZ]
            if step:
                wait_bytes(chunk, recv_wz.at[side, step - 1])
            chunk = w_all.at[(z + back) % NZ, rows]
            remote(
                chunk,
                chunk,
                send_wz.at[side, step],
                recv_wz.at[side, step],
                place(x, c, y, to),
            ).start()

    wait_bytes(w_all.at[z], recv_wy.at[0])
    ring_z(0)
    for side, source in ((0, yl), (1, yr)):
        wait_bytes(q_buf.at[source, pl.ds(4 - 4 * side, 4)], recv_y.at[side, 1 - side])
        wait_bytes(q_buf.at[y2, pl.ds(4 * side, 4)], recv_y.at[side, 2])

    lane = lax.broadcasted_iota(jnp.int32, (ROWS, 128), 1)
    row = lax.broadcasted_iota(jnp.int32, (ROWS, 128), 0)
    diagonal = lane == row
    stat_row = lax.broadcasted_iota(jnp.int32, (16, 128), 0)

    def finish(half):
        vectors = [[] for _ in range(NY)]
        for k in range(4):
            g = 4 * half + k
            total = acc[g, :, 128:]
            out = (acc[g, :, :128] / total).astype(jnp.bfloat16)
            level = peak[g] + jnp.log2(total)
            for part in range(NY):
                rows = slice(part * ROWS, (part + 1) * ROWS)
                vector = jnp.sum(jnp.where(diagonal, level[rows], 0.0), axis=0, keepdims=True)
                high = vector.astype(jnp.bfloat16).astype(jnp.float32)
                middle = (vector - high).astype(jnp.bfloat16).astype(jnp.float32)
                vectors[part] += [high, middle, vector - high - middle]
                o_part[part, half, k * ROWS : (k + 1) * ROWS] = out[rows]
        for part in range(NY):
            stats = jnp.zeros((16, 128), jnp.float32)
            for n, vector in enumerate(vectors[part]):
                stats = jnp.where(stat_row == n, vector, stats)
            o_part[part, half, 4 * ROWS :] = stats.astype(jnp.bfloat16)

    def partial_copy(half, d):
        to = (y + d) % NY
        return remote(
            o_part.at[to, half],
            o_recv.at[y, half],
            send_o.at[half, d - 1],
            recv_o.at[half, d - 1],
            place(x, c, to, z),
        )

    key_rows = NZ * TOK

    def stage(st, carry):
        p = (x + st + st // 2 - 2 * (st // 3)) % NX

        @pl.when(st == 1)
        def _():
            relay_x(1, v_buf)
            for ref, array in ((k_buf, 0), (v_buf, 1)):
                wait_bytes(ref.at[2 * xr], recv_x.at[array, 1, 0])

        @pl.when(st == 2)
        def _():
            ring_z(1)
            for ref, array in ((k_buf, 0), (v_buf, 1)):
                wait_bytes(ref.at[2 * xl + 1], recv_x.at[array, 0, 1])

        @pl.when(st == 3)
        def _():
            for ref, array in ((k_buf, 0), (v_buf, 1)):
                for side in range(2):
                    wait_bytes(ref.at[2 * x2 + side], recv_x.at[array, side, 2])
            lax.fori_loop(1, NQ, send_hidden, 0)
            pltpu.make_async_copy(
                hid_ref.at[:, own_columns(0)], hid_all.at[queue], recv_h.at[0]
            ).start()

        high, odd = p // 2, p % 2

        def both(j, carry):
            keys = k_buf[pl.ds(2 * p, 2)].reshape(2 * key_rows, DH)
            values = v_buf[pl.ds(2 * p, 2)].reshape(2 * key_rows, DH)
            attend([(2 * j, keys, values), (2 * j + 1, keys, values)], q_buf, acc, peak)
            return carry

        def halves(half, carry):
            same = 1 - (high - half) * (high - half)
            count = 2 * high * (1 - half) + odd * same
            lax.fori_loop(2 * half, 2 * half + count, both, 0)

            @pl.when(high == half)
            def _():
                keys = k_buf[pl.ds(2 * p, 2)].reshape(2 * key_rows, DH)
                values = v_buf[pl.ds(2 * p, 2)].reshape(2 * key_rows, DH)
                attend(
                    [
                        (2 * p, keys, values),
                        (2 * p + 1, keys[key_rows:], values[key_rows:]),
                    ],
                    q_buf,
                    acc,
                    peak,
                )

            @pl.when(st == 3)
            def _():
                finish(half)
                for d in (2, 1, 3):
                    partial_copy(half, d).start()

            return carry

        return lax.fori_loop(0, 2, halves, carry)

    lax.fori_loop(0, 4, stage, 0)
    ring_z(2)

    def column(vector):
        return jnp.sum(
            jnp.where(diagonal, jnp.broadcast_to(vector, (ROWS, 128)), 0.0),
            axis=1,
            keepdims=True,
        )

    def merge(half):
        refs = [o_part.at[y, half]] + [o_recv.at[(y + d) % NY, half] for d in (1, 2, 3)]
        stats = [ref[4 * ROWS :].astype(jnp.float32) for ref in refs]
        for k in range(4):
            g = 4 * half + k
            levels = [
                column(stat[3 * k : 3 * k + 1] + stat[3 * k + 1 : 3 * k + 2] + stat[3 * k + 2 : 3 * k + 3])
                for stat in stats
            ]
            top = functools.reduce(jnp.maximum, levels)
            shares = [jnp.exp2(level - top) for level in levels]
            total = functools.reduce(jnp.add, shares)
            mixed = functools.reduce(
                jnp.add,
                [
                    share * ref[k * ROWS : (k + 1) * ROWS].astype(jnp.float32)
                    for share, ref in zip(shares, refs)
                ],
            )
            merged[g] = (mixed / total).astype(jnp.bfloat16).reshape(2, TOK, DH)
        for k in range(4):
            g = 4 * half + k
            for n in range(2):
                zt = (x + 8 - g) % 4 + 4 * n

                @pl.when(zt != z)
                def _():
                    remote(
                        merged.at[g, n],
                        o_all.at[c, g, z],
                        send_z.at[0],
                        recv_z.at[half],
                        place(x, c, y, zt),
                    ).start()

                @pl.when(zt == z)
                def _():
                    pltpu.make_async_copy(
                        merged.at[g, n], o_all.at[c, g, z], recv_z.at[half]
                    ).start()

    def first(xs):
        return (xs + 8 - z) % 4

    def across(g, slot):
        return remote(
            o_all.at[c, g],
            o_all.at[c, g],
            send_c.at[slot],
            recv_c.at[slot],
            place(x, 1 - c, y, z),
        )

    for half in range(2):
        for d in (1, 3, 2):
            wait_bytes(o_recv.at[(y + NY - d) % NY, half], recv_o.at[half, d - 1])
        merge(half)
    for half in range(2):
        g = first(x) + 4 * half
        wait_bytes(o_all.at[c, g], recv_z.at[half])
        for d in (2, 1, 3):
            remote(
                o_all.at[c, g],
                o_all.at[c, g],
                send_g.at[half, d - 1],
                recv_g.at[half, d - 1],
                place((x + d) % NX, c, y, z),
            ).start()
        across(g, 4 * half).start()

    ring_z(3)
    wait_bytes(hid_all, recv_h.at[0])
    for side in range(2):
        wait_bytes(w_all.at[(z + 4) % NZ, pl.ds(2 * side, 2)], recv_wz.at[side, 3])

    token_lane = lax.broadcasted_iota(jnp.int32, (TOK, 128), 1)
    token_row = lax.broadcasted_iota(jnp.int32, (TOK, 128), 0)
    token_diagonal = token_lane == token_row
    last_row = lax.broadcasted_iota(jnp.int32, (8, 128), 0)

    def as_row(vector):
        return jnp.sum(
            jnp.where(token_diagonal, jnp.broadcast_to(vector, (TOK, 128)), 0.0),
            axis=0,
            keepdims=True,
        )

    def as_column(vector):
        return jnp.sum(
            jnp.where(token_diagonal, jnp.broadcast_to(vector, (TOK, 128)), 0.0),
            axis=1,
            keepdims=True,
        )

    for half in range(2):
        for d in (1, 3, 2):
            g = first((x + NX - d) % NX) + 4 * half
            wait_bytes(o_all.at[c, g], recv_g.at[half, d - 1])
            across(g, 4 * half + d).start()
        projected = None
        for parity in (c, 1 - c):
            if projected is not None:
                for d in range(NX):
                    g = first((x + NX - d) % NX) + 4 * half
                    wait_bytes(o_all.at[parity, g], recv_c.at[4 * half + d])
            for zh in range(0, NZ, 2):
                left = jnp.concatenate(
                    [
                        o_all[parity, 4 * half : 4 * half + 4, zh + k].reshape(4 * TOK, DH)
                        for k in range(2)
                    ],
                    axis=1,
                )
                right = jnp.concatenate(
                    [w_all[zh + k, 2 * parity + n] for k in range(2) for n in range(2)], axis=0
                )
                term = jnp.dot(left, right, preferred_element_type=jnp.float32)
                projected = term if projected is None else projected + term

        for g in range(4 * half, 4 * half + 4):
            rows = slice((g % 4) * TOK, (g % 4 + 1) * TOK)
            stream = hid_all[g].astype(jnp.float32) + consts[0, g : g + 1, :] * projected[rows]
            center = jnp.mean(stream, axis=1, keepdims=True)
            apart = stream - center
            spread = jnp.sum(apart * apart, axis=1, keepdims=True)
            scaled = (apart * consts[2, g : g + 1, :]).astype(jnp.bfloat16)
            mixed = lax.dot_general(
                scaled,
                final_buf[...],
                (((1,), (1,)), ((), ())),
                preferred_element_type=jnp.float32,
            )
            message[g, 0 : TOK // 2] = jnp.concatenate(
                [mixed[: TOK // 2], mixed[TOK // 2 :]], axis=1
            )
            both_sums = jnp.concatenate([sums[0, g : g + 1], sums[1, g : g + 1]], axis=1)
            message[g, TOK // 2 :] = jnp.where(
                last_row == 0,
                as_row(center),
                jnp.where(last_row == 1, as_row(spread), both_sums),
            )
        for g in range(4 * half, 4 * half + 4):
            for later in range(2 if g < NQ - 1 else 1):

                @pl.when(queue != g + later)
                def _():
                    remote(
                        message.at[g],
                        received.at[later, queue],
                        send_m.at[later, g],
                        recv_m.at[later, queue],
                        {"queue": g + later, "seq": seq},
                    ).start()

                @pl.when(queue == g + later)
                def _():
                    pltpu.make_async_copy(
                        message.at[g], received.at[later, queue], recv_m.at[later, queue]
                    ).start()

    def velocity_of(later):
        for source in range(NQ):
            wait_bytes(received.at[later, source], recv_m.at[later, source])
        tails = [received[later, source, TOK // 2 :] for source in range(NQ)]
        center = functools.reduce(jnp.add, [tail[0:1] for tail in tails]) / NQ
        spread = functools.reduce(jnp.add, [tail[1:2] for tail in tails])
        mixed = functools.reduce(
            jnp.add, [received[later, source, : TOK // 2] for source in range(NQ)]
        )
        mixed = jnp.concatenate([mixed[:, :LAT], mixed[:, LAT:]], axis=0)
        offset = functools.reduce(jnp.add, [tail[2:3, LAT:] for tail in tails])
        for tail in tails:
            away = tail[0:1] - center
            spread = spread + COLS * (away * away)
            mixed = mixed + as_column(away) * tail[2:3, :LAT]
        return mixed * as_column(1.0 / jnp.sqrt(spread / D + 1e-06)) + offset

    wait_bytes(hid_all.at[pl.ds(0, NQ - 1)], send_h.at[0])
    wait_bytes(act_all.at[pl.ds(0, NQ - 1)], send_h.at[1])
    for array in range(3):
        wait_bytes(q_buf.at[pl.ds(0, 3), pl.ds(0, 5), 0], send_a.at[array])

    @pl.when(xt != x)
    def _():
        wait_bytes(q_buf.at[0, 0, 0], send_a.at[3])

    @pl.when(queue < NQ - 1)
    def _():
        wait_bytes(lat_behind, send_h.at[2])

    for d in range(3):
        wait_bytes(w_all.at[0, 0], send_wy.at[d])
    for side in range(2):
        for array in range(2):
            for n in range(3):
                wait_bytes(k_buf.at[0], send_x.at[array, side, n])
        for n in range(3):
            wait_bytes(q_buf.at[0, pl.ds(0, 4)], send_y.at[side, n])
        for step in range(4):
            wait_bytes(w_all.at[0, pl.ds(0, NY if step < 3 else 2)], send_wz.at[side, step])
    for d in (1, 2, 3):
        for half in range(2):
            wait_bytes(o_part.at[0, 0], send_o.at[half, d - 1])
            wait_bytes(o_all.at[0, 0], send_g.at[half, d - 1])
    wait_bytes(merged.at[pl.ds(0, 7)], send_z.at[0])
    for slot in range(8):
        wait_bytes(o_all.at[0, 0], send_c.at[slot])
    for g in range(NQ):
        for later in range(2 if g < NQ - 1 else 1):

            @pl.when(queue != g + later)
            def _():
                wait_bytes(message.at[0], send_m.at[later, g])

    out_ref[:, 0:LAT] = velocity_of(0)

    @pl.when(queue == 0)
    def _():
        out_ref[:, LAT:] = fresh_buf[...]

    @pl.when(queue > 0)
    def _():
        velocity = velocity_of(1)
        wait_bytes(lat_behind, recv_h.at[2])
        out_ref[:, LAT:] = lat_behind[...] - STRIDE / 1000.0 * velocity


def fused(*operands):
    bf16, f32 = jnp.bfloat16, jnp.float32
    vmem, dma = pltpu.VMEM, pltpu.SemaphoreType.DMA
    in_specs = [pl.BlockSpec(memory_space=pl.ANY)] * 10
    in_specs[5] = pl.BlockSpec(memory_space=pltpu.SMEM)
    return pl.pallas_call(
        fused_kernel,
        out_shape=pltpu.VMEM((TOK, 2 * LAT), f32),
        in_specs=in_specs,
        out_specs=pl.BlockSpec(memory_space=pltpu.VMEM),
        scratch_shapes=[
            vmem((NQ, NZ, TOK, DH), bf16),
            vmem((NQ, NZ, TOK, DH), bf16),
            vmem((NY, NQ, 2, TOK, DH), bf16),
            vmem((NQ, NY * ROWS, 256), f32),
            vmem((NQ, NY * ROWS, 128), f32),
            vmem((NY, 2, PART, DH), bf16),
            vmem((NY, 2, PART, DH), bf16),
            vmem((NQ, 2, TOK, DH), bf16),
            vmem((NC, NQ, NZ, TOK, DH), bf16),
            vmem((NQ, TOK, COLS), bf16),
            vmem((NQ, 8, TEMB), f32),
            vmem((NZ, NY, 64, COLS), bf16),
            vmem((3, TEMB, COLS), bf16),
            vmem((LAT, COLS), bf16),
            vmem((TOK, LAT), f32),
            vmem((TOK, LAT), f32),
            vmem((3, NQ, COLS), f32),
            vmem((2, NQ, LAT), f32),
            vmem((NQ, MSG, 128), f32),
            vmem((2, NQ, MSG, 128), f32),
            dma((5,)),
            dma((4,)),
            dma((3,)),
            dma((3,)),
            dma((2, 4)),
            dma((2, 2, 3)),
            dma((2, 3)),
            dma((2, 3)),
            dma((1,)),
            dma((2, 3)),
            dma((8,)),
            dma((2, NQ)),
            dma((2,)),
            dma((2,)),
            dma((1,)),
            dma((3,)),
            dma((1,)),
            dma((2, 4)),
            dma((2, 2, 3)),
            dma((2, 3)),
            dma((2, 3)),
            dma((2,)),
            dma((2, 3)),
            dma((8,)),
            dma((2, NQ)),
        ],
        compiler_params=pltpu.CompilerParams(
            collective_id=0, has_side_effects=True, vmem_limit_bytes=60 * 1024 * 1024
        ),
        name="fused",
    )(*operands)


def body(
    hidden,
    queries,
    keys,
    values,
    timesteps,
    latents,
    fresh_noise,
    out_weight,
    mod_weight,
    final_weight,
):
    result = fused(
        queries[0],
        keys[0],
        values[0],
        hidden[0],
        out_weight,
        timesteps,
        mod_weight,
        final_weight.T,
        latents[0],
        fresh_noise,
    )
    return result[None, :, :LAT], result[None, :, LAT:]


def solution(mesh):
    placed = (
        P("queue", "seq", None),
        P("queue", "seq", None),
        P("queue", "seq", None),
        P("queue", "seq", None),
        P("queue"),
        P("queue", "seq", None),
        P("seq", None),
        P("seq", None),
        P(),
        P(),
    )
    return jax.shard_map(
        body,
        mesh=mesh,
        in_specs=placed,
        out_specs=(P("queue", "seq", None), P("queue", "seq", None)),
        check_vma=False,
    )
```
